32 devices in a mesh: gx: 2 (over y), gy: 4 (over x, core), off: 4 (over z).
Axes of the slice: x: 2, y: 2, z: 4, core: 2. Of those that a mesh axis runs over, the one named last changes fastest.
Arguments:
- volume: float32 [8, 256, 512], P(None, 'gx', 'gy'), may hold values from -3 to 3
- strength: float32 [8, 256, 512], P(None, 'gx', 'gy'), may hold values from 1 to 8
Outputs:
- denoised: float32 [8, 256, 512], P(None, 'gx', 'gy')
The draws below stay inside these ranges and needn't reach their ends.
All inputs are finite; a program needn't handle non-finite values.
Results may differ from the reference program's by a relative error of at most 0.00002.
Values sent between devices are 32-bit elements; how exact they have to be, the bound alone decides.
No kernel may reach another device: no remote copies, remote signals or barrier semaphores. Data moves between devices by JAX's collectives and lax.ppermute only.
A program may use at most 64 MiB of HBM per device.

```python
import math
import jax
import jax.numpy as jnp
from jax import lax

DEPTH = 8
NX = 256
NY = 512


def levels(key, extent, shards, least, largest):
    loudness = 1.0
    for dim, blocks in shards:
        heights = jax.random.uniform(jax.random.fold_in(jax.random.fold_in(key, 6), dim), (blocks,), jnp.float32, least / len(shards), largest / len(shards))
        loudness = loudness * jnp.repeat(jnp.exp(heights), extent[dim] // blocks).reshape((-1,) + (1,) * (len(extent) - 1 - dim))
    return loudness


def centred(rng, extent, width, limit, split=(), held_as=jnp.bfloat16):
    entries = width * jax.random.normal(rng, extent, jnp.float32)
    if split:
        entries = entries * levels(rng, extent, split, -0.22, 0.18)
    return jnp.clip(entries, -limit, limit).astype(held_as)


def setup_inputs(seed: int = 0) -> dict:
    seeds = jax.random.split(jax.random.key(seed), 3)
    volume = centred(seeds[0], (DEPTH, NX, NY), 1.0, 3.0, ((1, 2), (2, 4)), jnp.float32)
    strength = jnp.clip(jnp.exp(math.log(8.0) - 2.0794415 * jax.random.uniform(seeds[1], (DEPTH, NX, NY), jnp.float32) ** levels(seeds[1], (DEPTH, NX, NY), ((1, 2), (2, 4)), -0.2, 0.2)), 1.0, 8.0)
    return dict(volume=volume, strength=strength)


KERNEL_EDGE = math.exp(-0.5) / (1.0 + 2.0 * math.exp(-0.5))
KERNEL_MID = 1.0 / (1.0 + 2.0 * math.exp(-0.5))


def patch_weight(center_block, shifted, strength):
    difference = center_block - shifted
    squares = difference * difference
    squares = KERNEL_EDGE * (squares[:-2] + squares[2:]) + KERNEL_MID * squares[1:-1]
    squares = KERNEL_EDGE * (squares[:, :-2] + squares[:, 2:]) + KERNEL_MID * squares[:, 1:-1]
    squares = KERNEL_EDGE * (squares[:, :, :-2] + squares[:, :, 2:]) + KERNEL_MID * squares[:, :, 1:-1]
    weight = jnp.exp(-squares / strength)
    return weight, weight * shifted[1:-1, 1:-1, 1:-1]


def reference(volume, strength):
    depth, size_x, size_y = volume.shape
    padded = jnp.pad(volume, 3)
    center_block = padded[2:depth + 4, 2:size_x + 4, 2:size_y + 4]

    def one_turn(number, totals):
        number = jnp.asarray(number).astype(jnp.int32)
        shift_z = (number // 25 - 2 + 2).astype(jnp.int32)
        shift_x = ((number // 5) % 5 - 2 + 2).astype(jnp.int32)
        shift_y = (number % 5 - 2 + 2).astype(jnp.int32)
        shifted = lax.dynamic_slice(padded, (shift_z, shift_x, shift_y), (depth + 2, size_x + 2, size_y + 2))
        weight, values_here = patch_weight(center_block, shifted, strength)
        keep = number != 62
        weight = jnp.where(keep, weight, jnp.zeros_like(weight))
        values_here = jnp.where(keep, values_here, jnp.zeros_like(values_here))
        return (jnp.maximum(totals[0], weight), totals[1] + weight, totals[2] + values_here)

    empty = jnp.zeros(volume.shape, jnp.float32)
    top, total, weighted = lax.fori_loop(0, 125, one_turn, (empty, empty, empty))
    return (weighted + top * volume) / (total + top)
```

```python
import math

import jax
import jax.numpy as jnp
from jax import lax
from jax.experimental import pallas as pl
from jax.experimental.pallas import tpu as pltpu
from jax.sharding import PartitionSpec as P

EDGE = math.exp(-0.5) / (1.0 + 2.0 * math.exp(-0.5))
GAIN = math.exp(0.5)
SCALE = -(EDGE**3) * math.log2(math.e)
LANES = 128
SUBS = 8


def with_halo(cells, sides, width):
    for axis, dim in sides:
        count = lax.axis_size(axis)
        ends = count - 1
        head = lax.slice_in_dim(cells, 0, width, axis=dim)
        tail = lax.slice_in_dim(cells, cells.shape[dim] - width, cells.shape[dim], axis=dim)
        cells = jnp.concatenate(
            [
                lax.ppermute(tail, axis, [(i, (i + 1) % count) for i in range(ends)]),
                cells,
                lax.ppermute(head, axis, [((i + 1) % count, i) for i in range(ends)]),
            ],
            axis=dim,
        )
    return cells


def left(x, n):
    return x if n % LANES == 0 else pltpu.roll(x, (-n) % LANES, 1)


def right(x, n):
    return left(x, -n)


def lane_filter(x):
    return right(x, 1) + left(x, 1) + GAIN * x


def make_kernel(depth, rows, blocks):
    wide = blocks + 6

    def kernel(lower, upper, strength, out, vals, cent, energy, scale, top, total, weighted):
        base = lax.axis_index("off") * rows
        lane = lax.broadcasted_iota(jnp.int32, (SUBS, LANES), 1)

        def fill(z, _):
            windows = []
            for i in range(wide):
                at = pl.ds(base + i, SUBS, stride=blocks)
                low = lower[z, at, :]
                high = upper[z, at, :]
                vals[0, z, i] = low
                for c in range(1, 5):
                    vals[c, z, i] = jnp.where(lane < LANES - c, left(low, c), left(high, c))
                windows.append(jnp.where(lane < 2, left(low, 126), right(high, 2)))
            for i in range(blocks + 2):
                cent[0, z, i] = -2.0 * vals[2, z, i + 2]
            strips = []
            for i in range(wide):
                strip = jnp.zeros((SUBS, LANES), jnp.float32)
                for c in range(5):
                    strip = jnp.where(
                        (lane >= 1 + 4 * c) & (lane < 5 + 4 * c), right(windows[i], 1 + 3 * c), strip
                    )
                strips.append(strip)
            for i in range(blocks + 2):
                packed = jnp.zeros((SUBS, LANES), jnp.float32)
                for b in range(5):
                    packed = jnp.where(
                        (lane >= 1 + 20 * b) & (lane < 21 + 20 * b), right(strips[i + b], 20 * b), packed
                    )
                vals[5, z, i] = packed
                spread = jnp.where((lane >= 1) & (lane < 5), left(windows[i + 2], 1), 0.0)
                for n in (4, 8, 16, 32, 64):
                    spread = spread + right(spread, n)
                cent[1, z, i] = -2.0 * spread
            for i in range(blocks):
                s = strength[z, pl.ds(base + i, SUBS, stride=blocks), :]
                s = SCALE / s
                scale[0, z, i] = right(s, 1)
                spread = jnp.where((lane == 2) | (lane == 3), left(s, 124), 0.0)
                for n in (4, 8, 16, 32, 64):
                    spread = spread + right(spread, n)
                scale[1, z, i] = spread
            for i in range(blocks):
                for kind in range(2):
                    top[kind, z, i] = jnp.zeros((SUBS, LANES), jnp.float32)
                    total[kind, z, i] = jnp.zeros((SUBS, LANES), jnp.float32)
                    weighted[kind, z, i] = jnp.zeros((SUBS, LANES), jnp.float32)
            return 0

        lax.fori_loop(0, depth, fill, 0)

        def energies(plane, _):
            count = blocks + 4
            filtered = []
            for z in range(depth):
                squares = []
                for i in range(wide):
                    v = vals[plane, z, i]
                    squares.append(v * v)
                filtered.append(
                    [
                        lane_filter(squares[i] + squares[i + 2] + GAIN * squares[i + 1])
                        for i in range(count)
                    ]
                )
                if z >= 1:
                    store_energy(plane, z - 1, filtered)
                if z == 0:
                    for i in range(count):
                        energy[plane, 0, i] = filtered[0][i]
            store_energy(plane, depth - 1, filtered)
            for i in range(count):
                energy[plane, depth + 1, i] = filtered[depth - 1][i]
            return 0

        def store_energy(plane, z, filtered):
            for i in range(blocks + 4):
                e = GAIN * filtered[z][i]
                if z > 0:
                    e = e + filtered[z - 1][i]
                if z < depth - 1:
                    e = e + filtered[z + 1][i]
                energy[plane, z + 1, i] = e

        for i in range(blocks + 2, wide):
            for z in range(depth):
                vals[5, z, i] = jnp.zeros((SUBS, LANES), jnp.float32)
        lax.fori_loop(0, 6, energies, 0)

        def offset(a, plane, b, kind, mask=None):
            first, last = max(0, -a), min(depth, depth - a)
            filtered = {}

            def emit(z):
                if not first <= z < last:
                    return
                p = [cent[kind, z, i] * vals[plane, z + a, i + b] for i in range(blocks + 2)]
                filtered[z] = [
                    lane_filter(p[i] + p[i + 2] + GAIN * p[i + 1]) for i in range(blocks)
                ]

            emit(0)
            for z in range(depth):
                emit(z + 1)
                for i in range(blocks):
                    parts = [filtered[y][i] for y in (z - 1, z + 1) if y in filtered]
                    if z in filtered:
                        parts.append(GAIN * filtered[z][i])
                    if -1 <= z + a <= depth:
                        parts.append(energy[plane, z + a + 1, i + b])
                    if parts:
                        e = parts[0]
                        for part in parts[1:]:
                            e = e + part
                        w = jnp.exp2(scale[kind, z, i] * e)
                    else:
                        w = jnp.ones((SUBS, LANES), jnp.float32)
                    if mask is not None:
                        w = jnp.where(mask, 0.0, w)
                    top[kind, z, i] = jnp.maximum(top[kind, z, i], w)
                    total[kind, z, i] += w
                    if 0 <= z + a < depth:
                        weighted[kind, z, i] += w * vals[plane, z + a, i + b + 1]

        for a in range(-2, 3):
            skip = a == 0

            def one(n, _, a=a, skip=skip):
                if skip:
                    n = n + jnp.where(n >= 12, 1, 0)
                offset(a, n % 5, n // 5, 0)
                return 0

            lax.fori_loop(0, 24 if skip else 25, one, 0)
            offset(a, 5, 0, 1, mask=(lane >= 49) & (lane < 53) if skip else None)

        def finish(z, _):
            def ratio(t, s, w, v):
                return (w + t * v) / (s + t)

            for i in range(blocks):
                main = ratio(top[0, z, i], total[0, z, i], weighted[0, z, i], vals[2, z, i + 3])
                keep = (lane >= 1) & (lane < 101)
                t = jnp.where(keep, top[1, z, i], 0.0)
                s = jnp.where(keep, total[1, z, i], 0.0)
                w = jnp.where(keep, weighted[1, z, i], 0.0)
                for n in (64, 32, 16, 8, 4):
                    t = jnp.maximum(t, left(t, n))
                    s = s + left(s, n)
                    w = w + left(w, n)
                edge = ratio(t, s, w, -0.5 * cent[1, z, i + 1])
                out[z, pl.ds(i, SUBS, stride=blocks), :] = jnp.where(
                    lane < LANES - 2, left(main, 1), edge
                )
            return 0

        lax.fori_loop(0, depth, finish, 0)

    return kernel


def denoise(extended, strength):
    depth, size_x, size_y = strength.shape
    rows = size_x // lax.axis_size("off")
    blocks = rows // SUBS
    assert size_y == LANES
    tile = (SUBS, LANES)
    f32 = jnp.float32
    lower = extended[:, :, :LANES]
    upper = jnp.pad(extended[:, :, LANES:], ((0, 0), (0, 0), (0, LANES - 6)))
    return pl.pallas_call(
        make_kernel(depth, rows, blocks),
        out_shape=jax.ShapeDtypeStruct((depth, rows, size_y), f32),
        in_specs=[pl.BlockSpec(memory_space=pltpu.VMEM)] * 3,
        out_specs=pl.BlockSpec(memory_space=pltpu.VMEM),
        scratch_shapes=[
            pltpu.VMEM((6, depth, blocks + 6) + tile, f32),
            pltpu.VMEM((2, depth, blocks + 2) + tile, f32),
            pltpu.VMEM((6, depth + 2, blocks + 4) + tile, f32),
            pltpu.VMEM((2, depth, blocks) + tile, f32),
            pltpu.VMEM((2, depth, blocks) + tile, f32),
            pltpu.VMEM((2, depth, blocks) + tile, f32),
            pltpu.VMEM((2, depth, blocks) + tile, f32),
        ],
        compiler_params=pltpu.CompilerParams(vmem_limit_bytes=32 * 2**20),
    )(lower, upper, strength)


def shards(volume, strength):
    extended = with_halo(volume, (("gx", 1), ("gy", 2)), 3)
    part = denoise(extended, strength)
    return lax.all_gather(part, "off", axis=1, tiled=True)


def solution(mesh):
    return jax.shard_map(
        shards,
        mesh=mesh,
        in_specs=(P(None, "gx", "gy"), P(None, "gx", "gy")),
        out_specs=P(None, "gx", "gy"),
        check_vma=False,
    )
```

```python
import math

import jax
import jax.numpy as jnp
from jax import lax
from jax.experimental import pallas as pl
from jax.experimental.pallas import tpu as pltpu
from jax.sharding import PartitionSpec as P

EDGE = math.exp(-0.5) / (1.0 + 2.0 * math.exp(-0.5))
GAIN = math.exp(0.5)
SCALE = -(EDGE**3) * math.log2(math.e)
LANES = 128
SUBS = 8


def with_halo(cells, sides, width):
    for axis, dim in sides:
        count = lax.axis_size(axis)
        ends = count - 1
        head = lax.slice_in_dim(cells, 0, width, axis=dim)
        tail = lax.slice_in_dim(cells, cells.shape[dim] - width, cells.shape[dim], axis=dim)
        cells = jnp.concatenate(
            [
                lax.ppermute(tail, axis, [(i, (i + 1) % count) for i in range(ends)]),
                cells,
                lax.ppermute(head, axis, [((i + 1) % count, i) for i in range(ends)]),
            ],
            axis=dim,
        )
    return cells


def make_kernel(depth, rows, blocks):
    wide = blocks + 6
    tall = -(-(rows + 6) // SUBS)

    def kernel(middle, sides, strength, out, flat, vals, cent, energy, scale, top, total, weighted):
        lane = lax.broadcasted_iota(jnp.int32, (SUBS, LANES), 1)

        def fill(z, _):
            for r in range(tall):
                at = pl.ds(SUBS * r, SUBS)
                v, h = middle[z, at, :], sides[z, at, :]
                flat[3, at, :] = v
                for c in range(1, 4):
                    flat[3 + c, at, :] = pltpu.roll(jnp.where(lane < c, h, v), LANES - c, 1)
                    flat[3 - c, at, :] = pltpu.roll(jnp.where(lane >= LANES - c, h, v), c, 1)
            for i in range(wide):
                for c in range(7):
                    v = flat[c, pl.ds(i, SUBS, stride=blocks), :]
                    vals[c, z, i] = v
                    if 2 <= c <= 4 and 2 <= i < wide - 2:
                        cent[c - 2, z, i - 2] = (-2.0 * GAIN if c == 3 else -2.0) * v
            for i in range(blocks):
                scale[z, i] = SCALE / strength[z, pl.ds(i, SUBS, stride=blocks), :]
                top[z, i] = jnp.zeros((SUBS, LANES), jnp.float32)
                total[z, i] = jnp.zeros((SUBS, LANES), jnp.float32)
                weighted[z, i] = jnp.zeros((SUBS, LANES), jnp.float32)
            return 0

        lax.fori_loop(0, depth, fill, 0)

        def three(a, b, c):
            return a + c + GAIN * b

        def energies(c, _):
            count = blocks + 4
            filtered = []

            def store(z):
                for i in range(count):
                    e = GAIN * filtered[z][i] if 0 <= z < depth else None
                    for y in (z - 1, z + 1):
                        if 0 <= y < depth:
                            e = filtered[y][i] if e is None else e + filtered[y][i]
                    energy[c, z + 1, i] = e

            for z in range(depth):
                line = []
                for i in range(wide):
                    u, v, w = (vals[c + k, z, i] for k in range(3))
                    line.append(three(u * u, v * v, w * w))
                filtered.append([three(*line[i : i + 3]) for i in range(count)])
                store(z - 1)
            store(depth - 1)
            store(depth)
            return 0

        lax.fori_loop(0, 5, energies, 0)

        def offsets(a, b, group):
            first, last = max(0, -a), min(depth, depth - a)
            planes = sorted({c + k for c in group for k in range(3)})
            filtered = {}

            def emit(z):
                if not first <= z < last:
                    return
                lines = {c: [] for c in group}
                for i in range(blocks + 2):
                    v = {k: vals[k, z + a, i + b] for k in planes}
                    m = [cent[k, z, i] for k in range(3)]
                    for c in group:
                        lines[c].append(m[0] * v[c] + m[2] * v[c + 2] + m[1] * v[c + 1])
                filtered[z] = {
                    c: [three(*lines[c][i : i + 3]) for i in range(blocks)] for c in group
                }

            emit(0)
            for z in range(depth):
                emit(z + 1)
                for i in range(blocks):
                    weights = {}
                    for c in group:
                        parts = [filtered[y][c][i] for y in (z - 1, z + 1) if y in filtered]
                        if z in filtered:
                            parts.append(GAIN * filtered[z][c][i])
                        if -1 <= z + a <= depth:
                            parts.append(energy[c, z + a + 1, i + b])
                        if parts:
                            weights[c] = jnp.exp2(scale[z, i] * sum(parts[1:], parts[0]))
                        else:
                            weights[c] = jnp.ones((SUBS, LANES), jnp.float32)
                    t = top[z, i]
                    s = total[z, i]
                    for c in group:
                        t = jnp.maximum(t, weights[c])
                        s = s + weights[c]
                    top[z, i] = t
                    total[z, i] = s
                    if 0 <= z + a < depth:
                        w = weighted[z, i]
                        for c in group:
                            w = w + weights[c] * vals[c + 1, z + a, i + b + 1]
                        weighted[z, i] = w

        for a in range(-2, 3):

            def one(n, _, a=a):
                b = n + jnp.where(n >= 2, 1, 0) if a == 0 else n
                offsets(a, b, range(5))
                return 0

            lax.fori_loop(0, 4 if a == 0 else 5, one, 0)
        offsets(0, 2, (0, 1, 3, 4))

        def finish(z, _):
            for i in range(blocks):
                t = top[z, i]
                out[z, pl.ds(i, SUBS, stride=blocks), :] = (
                    weighted[z, i] + t * vals[3, z, i + 3]
                ) / (total[z, i] + t)
            return 0

        lax.fori_loop(0, depth, finish, 0)

    return kernel


def denoise(extended, strength):
    depth, size_x, size_y = strength.shape
    rows = size_x // lax.axis_size("off")
    blocks = rows // SUBS
    tall = -(-(rows + 6) // SUBS) * SUBS
    assert size_y == LANES
    start = lax.axis_index("off") * rows
    strength = lax.dynamic_slice_in_dim(strength, start, rows, 1)
    mine = lax.dynamic_slice_in_dim(extended, start, rows + 6, 1)
    mine = jnp.pad(mine, ((0, 0), (0, tall - rows - 6), (0, 0)))
    middle = mine[:, :, 3 : LANES + 3]
    sides = jnp.concatenate(
        [
            mine[:, :, LANES + 3 :],
            jnp.zeros((depth, tall, LANES - 6), jnp.float32),
            mine[:, :, :3],
        ],
        axis=2,
    )
    tile = (SUBS, LANES)
    f32 = jnp.float32
    return pl.pallas_call(
        make_kernel(depth, rows, blocks),
        out_shape=jax.ShapeDtypeStruct((depth, rows, size_y), f32),
        in_specs=[pl.BlockSpec(memory_space=pltpu.VMEM)] * 3,
        out_specs=pl.BlockSpec(memory_space=pltpu.VMEM),
        scratch_shapes=[
            pltpu.VMEM((7, tall, LANES), f32),
            pltpu.VMEM((7, depth, blocks + 6) + tile, f32),
            pltpu.VMEM((3, depth, blocks + 2) + tile, f32),
            pltpu.VMEM((5, depth + 2, blocks + 4) + tile, f32),
            pltpu.VMEM((depth, blocks) + tile, f32),
            pltpu.VMEM((depth, blocks) + tile, f32),
            pltpu.VMEM((depth, blocks) + tile, f32),
            pltpu.VMEM((depth, blocks) + tile, f32),
        ],
        compiler_params=pltpu.CompilerParams(vmem_limit_bytes=32 * 2**20),
    )(middle, sides, strength)


def shards(volume, strength):
    extended = with_halo(volume, (("gx", 1), ("gy", 2)), 3)
    part = denoise(extended, strength)
    return lax.all_gather(part, "off", axis=1, tiled=True)


def solution(mesh):
    return jax.shard_map(
        shards,
        mesh=mesh,
        in_specs=(P(None, "gx", "gy"), P(None, "gx", "gy")),
        out_specs=P(None, "gx", "gy"),
        check_vma=False,
    )
```

```python
import math

import jax
import jax.numpy as jnp
from jax import lax
from jax.experimental import pallas as pl
from jax.experimental.pallas import tpu as pltpu
from jax.sharding import PartitionSpec as P

EDGE = math.exp(-0.5) / (1.0 + 2.0 * math.exp(-0.5))
GAIN = math.exp(0.5)
SCALE = -(EDGE**3) * math.log2(math.e)
LANES = 128
SUBS = 8
VMEM = pl.BlockSpec(memory_space=pltpu.VMEM)


def partners(count):
    assert count % 2 == 0
    first = [i ^ 1 for i in range(count)]
    second = [(((i + 1) ^ 1) - 1) % count for i in range(count)]
    return first, second


def pack_kernel(rows):
    blocks = rows // SUBS + 2

    def kernel(volume, strips, corner, layer):
        depth, size_x, _ = volume.shape
        off = lax.axis_index("off")
        lane = lax.broadcasted_iota(jnp.int32, (SUBS, LANES), 1)
        place = (lane + 3) % LANES

        def packed(start):
            line = jnp.zeros((SUBS, LANES), jnp.float32)
            for z in range(depth):
                v = volume[z, pl.ds(start, SUBS), :]
                v = pltpu.roll(v, 16 * z, 1) if z else v
                line = jnp.where((place >= 16 * z) & (place < 16 * z + 6), v, line)
            return line

        for j in range(blocks):
            at = jnp.clip(off * rows + SUBS * (j - 1), 0, size_x - SUBS)
            strips[pl.ds(SUBS * j, SUBS), :] = packed(pl.multiple_of(at, SUBS))
        at = pl.multiple_of(jnp.where(off == 0, size_x - SUBS, 0), SUBS)
        corner[...] = packed(at)
        for z in range(depth):
            layer[z] = volume[z, pl.ds(at, SUBS), :]

    return kernel


def make_kernel(depth, rows, blocks):
    wide = blocks + 6
    tall = rows // SUBS + 2

    def kernel(
        volume, strength, layer, near, far, near_corner, far_corner,
        out, flat, vals, cent, energy, scale, top, total, weighted,
    ):
        lane = lax.broadcasted_iota(jnp.int32, (SUBS, LANES), 1)
        size_x = volume.shape[1]
        off, offs = lax.axis_index("off"), lax.axis_size("off")
        gx, gxs = lax.axis_index("gx"), lax.axis_size("gx")
        gy, gys = lax.axis_index("gy"), lax.axis_size("gy")
        start = off * rows
        odd = gy % 2 == 1
        outer = lane % 16 >= 13
        closed = (outer & (gy == 0)) | ((lane % 16 < 3) & (gy == gys - 1))
        from_near = outer == odd
        ends = {0: (off == 0, gx == 0), tall - 1: (off == offs - 1, gx == gxs - 1)}

        def side(j):
            at = pl.ds(SUBS * j, SUBS)
            line = jnp.where(from_near, near[at, :], far[at, :])
            if j in ends:
                corner = jnp.where(from_near, near_corner[...], far_corner[...])
                corner = jnp.where(ends[j][1], 0.0, corner)
                line = jnp.where(ends[j][0], corner, line)
            return jnp.where(closed, 0.0, line)

        lines = [side(j) for j in range(tall)]

        def fill(z, _):
            for r in range(tall):
                at = pl.ds(SUBS * r, SUBS)
                here = jnp.clip(start + SUBS * (r - 1), 0, size_x - SUBS)
                v = volume[z, pl.ds(pl.multiple_of(here, SUBS), SUBS), :]
                if r in ends:
                    v = jnp.where(ends[r][0], jnp.where(ends[r][1], 0.0, layer[z]), v)
                h = pltpu.roll(lines[r], LANES - 16 * z, 1)
                flat[3, at, :] = v
                for c in range(1, 4):
                    flat[3 + c, at, :] = pltpu.roll(jnp.where(lane < c, h, v), LANES - c, 1)
                    flat[3 - c, at, :] = pltpu.roll(jnp.where(lane >= LANES - c, h, v), c, 1)
            for i in range(wide):
                for c in range(7):
                    v = flat[c, pl.ds(SUBS - 3 + i, SUBS, stride=blocks), :]
                    vals[c, z, i] = v
                    if 2 <= c <= 4 and 2 <= i < wide - 2:
                        cent[c - 2, z, i - 2] = (-2.0 * GAIN if c == 3 else -2.0) * v
            for i in range(blocks):
                s = strength[z, pl.ds(start + i, SUBS, stride=blocks), :]
                scale[z, i] = SCALE / s
                top[z, i] = jnp.zeros((SUBS, LANES), jnp.float32)
                total[z, i] = jnp.zeros((SUBS, LANES), jnp.float32)
                weighted[z, i] = jnp.zeros((SUBS, LANES), jnp.float32)
            return 0

        for z in range(depth):
            fill(z, 0)

        def three(a, b, c):
            return a + c + GAIN * b

        def energies(c, _):
            count = blocks + 4
            filtered = []

            def store(z):
                for i in range(count):
                    e = GAIN * filtered[z][i] if 0 <= z < depth else None
                    for y in (z - 1, z + 1):
                        if 0 <= y < depth:
                            e = filtered[y][i] if e is None else e + filtered[y][i]
                    energy[c, z + 1, i] = e

            for z in range(depth):
                line = []
                for i in range(wide):
                    u, v, w = (vals[c + k, z, i] for k in range(3))
                    line.append(three(u * u, v * v, w * w))
                filtered.append([three(*line[i : i + 3]) for i in range(count)])
                store(z - 1)
            store(depth - 1)
            store(depth)
            return 0

        lax.fori_loop(0, 5, energies, 0)

        def offsets(a, b, group):
            first, last = max(0, -a), min(depth, depth - a)
            planes = sorted({c + k for c in group for k in range(3)})
            filtered = {}

            def emit(z):
                if not first <= z < last:
                    return
                lines = {c: [] for c in group}
                for i in range(blocks + 2):
                    v = {k: vals[k, z + a, i + b] for k in planes}
                    m = [cent[k, z, i] for k in range(3)]
                    for c in group:
                        lines[c].append(m[0] * v[c] + m[2] * v[c + 2] + m[1] * v[c + 1])
                filtered[z] = {
                    c: [three(*lines[c][i : i + 3]) for i in range(blocks)] for c in group
                }

            emit(0)
            for z in range(depth):
                emit(z + 1)
                for i in range(blocks):
                    weights = {}
                    for c in group:
                        parts = [filtered[y][c][i] for y in (z - 1, z + 1) if y in filtered]
                        if z in filtered:
                            parts.append(GAIN * filtered[z][c][i])
                        if -1 <= z + a <= depth:
                            parts.append(energy[c, z + a + 1, i + b])
                        if parts:
                            weights[c] = jnp.exp2(scale[z, i] * sum(parts[1:], parts[0]))
                        else:
                            weights[c] = jnp.ones((SUBS, LANES), jnp.float32)
                    t = top[z, i]
                    s = total[z, i]
                    for c in group:
                        t = jnp.maximum(t, weights[c])
                        s = s + weights[c]
                    top[z, i] = t
                    total[z, i] = s
                    if 0 <= z + a < depth:
                        w = weighted[z, i]
                        for c in group:
                            w = w + weights[c] * vals[c + 1, z + a, i + b + 1]
                        weighted[z, i] = w

        for a in range(-2, 3):

            def one(n, _, a=a):
                b = n + jnp.where(n >= 2, 1, 0) if a == 0 else n
                offsets(a, b, range(5))
                return 0

            lax.fori_loop(0, 4 if a == 0 else 5, one, 0)
        offsets(0, 2, (0, 1, 3, 4))

        def finish(z, _):
            for i in range(blocks):
                t = top[z, i]
                out[z, pl.ds(i, SUBS, stride=blocks), :] = (
                    weighted[z, i] + t * vals[3, z, i + 3]
                ) / (total[z, i] + t)
            return 0

        lax.fori_loop(0, depth, finish, 0)

    return kernel


def denoise(volume, strength):
    depth, size_x, size_y = strength.shape
    sizes = {axis: lax.axis_size(axis) for axis in ("gx", "gy", "off")}
    gxs, gys, offs = sizes["gx"], sizes["gy"], sizes["off"]
    rows = size_x // offs
    blocks = rows // SUBS
    tall = rows + 2 * SUBS
    assert size_y == LANES and offs > 1
    tile = (SUBS, LANES)
    f32 = jnp.float32
    strips, corner, layer = pl.pallas_call(
        pack_kernel(rows),
        out_shape=[
            jax.ShapeDtypeStruct((tall, LANES), f32),
            jax.ShapeDtypeStruct(tile, f32),
            jax.ShapeDtypeStruct((depth,) + tile, f32),
        ],
        in_specs=[VMEM],
        out_specs=[VMEM] * 3,
    )(volume)

    def across(swap):
        moves = []
        for x in range(gxs):
            for y in range(gys):
                for k in range(offs):
                    to = (x + (1 if k == 0 else -1)) % gxs
                    moves.append(((x * gys + y) * offs + k, (to * gys + swap[y]) * offs + k))
        return moves

    axes = ("gx", "gy", "off")
    first, second = partners(gys)
    near = lax.ppermute(strips, "gy", list(enumerate(first)))
    far = lax.ppermute(strips, "gy", list(enumerate(second)))
    layer = lax.ppermute(layer, axes, across(list(range(gys))))
    near_corner = lax.ppermute(corner, axes, across(first))
    far_corner = lax.ppermute(corner, axes, across(second))
    return pl.pallas_call(
        make_kernel(depth, rows, blocks),
        out_shape=jax.ShapeDtypeStruct((depth, rows, size_y), f32),
        in_specs=[VMEM] * 7,
        out_specs=VMEM,
        scratch_shapes=[
            pltpu.VMEM((7, tall, LANES), f32),
            pltpu.VMEM((7, depth, blocks + 6) + tile, f32),
            pltpu.VMEM((3, depth, blocks + 2) + tile, f32),
            pltpu.VMEM((5, depth + 2, blocks + 4) + tile, f32),
            pltpu.VMEM((depth, blocks) + tile, f32),
            pltpu.VMEM((depth, blocks) + tile, f32),
            pltpu.VMEM((depth, blocks) + tile, f32),
            pltpu.VMEM((depth, blocks) + tile, f32),
        ],
        compiler_params=pltpu.CompilerParams(vmem_limit_bytes=32 * 2**20),
    )(volume, strength, layer, near, far, near_corner, far_corner)


def gathered(part):
    depth, rows, size_y = part.shape
    count = lax.axis_size("off")
    off = lax.axis_index("off")
    whole = jnp.zeros((count, depth, rows, size_y), part.dtype)
    whole = lax.dynamic_update_slice(whole, part[None], (off, 0, 0, 0))
    for step in range(1, count):
        moves = [(i, i ^ step) for i in range(count)]
        other = lax.ppermute(part, "off", moves)
        whole = lax.dynamic_update_slice(whole, other[None], (off ^ step, 0, 0, 0))
    return jnp.swapaxes(whole, 0, 1).reshape(depth, count * rows, size_y)


def shards(volume, strength):
    return gathered(denoise(volume, strength))


def solution(mesh):
    return jax.shard_map(
        shards,
        mesh=mesh,
        in_specs=(P(None, "gx", "gy"), P(None, "gx", "gy")),
        out_specs=P(None, "gx", "gy"),
        check_vma=False,
    )
```

```python
import math

import jax
import jax.numpy as jnp
from jax import lax
from jax.experimental import pallas as pl
from jax.experimental.pallas import tpu as pltpu
from jax.sharding import PartitionSpec as P

EDGE = math.exp(-0.5) / (1.0 + 2.0 * math.exp(-0.5))
GAIN = math.exp(0.5)
SCALE = -(EDGE**3) * math.log2(math.e)
LANES = 128
SUBS = 8
VMEM = pl.BlockSpec(memory_space=pltpu.VMEM)


def partners(count):
    assert count % 2 == 0
    first = [i ^ 1 for i in range(count)]
    second = [(((i + 1) ^ 1) - 1) % count for i in range(count)]
    return first, second


def pack_kernel(rows):
    blocks = rows // SUBS + 2

    def kernel(volume, strips, corner, layer):
        depth, size_x, _ = volume.shape
        off = lax.axis_index("off")
        lane = lax.broadcasted_iota(jnp.int32, (SUBS, LANES), 1)
        place = (lane + 3) % LANES

        def packed(start):
            line = jnp.zeros((SUBS, LANES), jnp.float32)
            for z in range(depth):
                v = volume[z, pl.ds(start, SUBS), :]
                v = pltpu.roll(v, 16 * z, 1) if z else v
                line = jnp.where((place >= 16 * z) & (place < 16 * z + 6), v, line)
            return line

        for j in range(blocks):
            at = jnp.clip(off * rows + SUBS * (j - 1), 0, size_x - SUBS)
            strips[pl.ds(SUBS * j, SUBS), :] = packed(pl.multiple_of(at, SUBS))
        at = pl.multiple_of(jnp.where(off == 0, size_x - SUBS, 0), SUBS)
        corner[...] = packed(at)
        for z in range(depth):
            layer[z] = volume[z, pl.ds(at, SUBS), :]

    return kernel


def three(a, b, c):
    return a + c + GAIN * b


def prepare_kernel(depth, rows, blocks, slices):
    wide = blocks + 6
    tall = rows // SUBS + 2

    def kernel(
        volume, strength, layer, near, far, near_corner, far_corner,
        out, vals, cent, energy, scale, flat, mine, arrived, *sums,
    ):
        lane = lax.broadcasted_iota(jnp.int32, (SUBS, LANES), 1)
        size_x = volume.shape[1]
        off, offs = lax.axis_index("off"), lax.axis_size("off")
        gx, gxs = lax.axis_index("gx"), lax.axis_size("gx")
        gy, gys = lax.axis_index("gy"), lax.axis_size("gy")
        start = pl.multiple_of(off * rows, rows)
        fetch = pltpu.make_async_copy(strength.at[:, pl.ds(start, rows), :], mine, arrived)
        fetch.start()
        odd = gy % 2 == 1
        outer = lane % 16 >= 13
        closed = (outer & (gy == 0)) | ((lane % 16 < 3) & (gy == gys - 1))
        from_near = outer == odd
        ends = {0: (off == 0, gx == 0), tall - 1: (off == offs - 1, gx == gxs - 1)}

        def side(j):
            at = pl.ds(SUBS * j, SUBS)
            line = jnp.where(from_near, near[at, :], far[at, :])
            if j in ends:
                corner = jnp.where(from_near, near_corner[...], far_corner[...])
                corner = jnp.where(ends[j][1], 0.0, corner)
                line = jnp.where(ends[j][0], corner, line)
            return jnp.where(closed, 0.0, line)

        lines = [side(j) for j in range(tall)]

        def fill(z):
            for r in range(tall):
                at = pl.ds(SUBS * r, SUBS)
                here = jnp.clip(start + SUBS * (r - 1), 0, size_x - SUBS)
                v = volume[z, pl.ds(pl.multiple_of(here, SUBS), SUBS), :]
                if r in ends:
                    v = jnp.where(ends[r][0], jnp.where(ends[r][1], 0.0, layer[z]), v)
                h = pltpu.roll(lines[r], LANES - 16 * z, 1)
                flat[3, at, :] = v
                for c in range(1, 4):
                    flat[3 + c, at, :] = pltpu.roll(jnp.where(lane < c, h, v), LANES - c, 1)
                    flat[3 - c, at, :] = pltpu.roll(jnp.where(lane >= LANES - c, h, v), c, 1)
            for i in range(wide):
                for c in range(7):
                    v = flat[c, pl.ds(SUBS - 3 + i, SUBS, stride=blocks), :]
                    vals[c, z, i] = v
                    if 2 <= c <= 4 and 2 <= i < wide - 2:
                        cent[c - 2, z, i - 2] = (-2.0 * GAIN if c == 3 else -2.0) * v

        for z in range(depth):
            fill(z)

        def energies(c, _):
            count = blocks + 4
            filtered = []

            def store(z):
                for i in range(count):
                    e = GAIN * filtered[z][i] if 0 <= z < depth else None
                    for y in (z - 1, z + 1):
                        if 0 <= y < depth:
                            e = filtered[y][i] if e is None else e + filtered[y][i]
                    energy[c, z + 1, i] = e

            for z in range(depth):
                line = []
                for i in range(wide):
                    u, v, w = (vals[c + k, z, i] for k in range(3))
                    line.append(three(u * u, v * v, w * w))
                filtered.append([three(*line[i : i + 3]) for i in range(count)])
                store(z - 1)
            store(depth - 1)
            store(depth)
            return 0

        lax.fori_loop(0, 5, energies, 0)

        fetch.wait()
        for z in range(depth):
            for i in range(blocks):
                scale[z, i] = SCALE / mine[z, pl.ds(i, SUBS, stride=blocks), :]

        weigh(depth, blocks, slices, vals, cent, energy, scale, out, *sums)

    return kernel


def weigh(depth, blocks, slices, vals, cent, energy, scale, out, top, total, weighted):
    begin, end = slices
    for z in range(end - begin):
        for i in range(blocks):
            for ref in (top, total, weighted):
                ref[z, i] = jnp.zeros((SUBS, LANES), jnp.float32)

    def offsets(a, b, group):
        first, last = max(0, -a, begin - 1), min(depth, depth - a, end + 1)
        planes = sorted({c + k for c in group for k in range(3)})
        filtered = {}

        def emit(z):
            if not first <= z < last:
                return
            lines = {c: [] for c in group}
            for i in range(blocks + 2):
                v = {k: vals[k, z + a, i + b] for k in planes}
                m = [cent[k, z, i] for k in range(3)]
                for c in group:
                    lines[c].append(m[0] * v[c] + m[2] * v[c + 2] + m[1] * v[c + 1])
            filtered[z] = {
                c: [three(*lines[c][i : i + 3]) for i in range(blocks)] for c in group
            }

        emit(begin - 1)
        emit(begin)
        for z in range(begin, end):
            emit(z + 1)
            for i in range(blocks):
                weights = {}
                for c in group:
                    parts = [filtered[y][c][i] for y in (z - 1, z + 1) if y in filtered]
                    if z in filtered:
                        parts.append(GAIN * filtered[z][c][i])
                    if -1 <= z + a <= depth:
                        parts.append(energy[c, z + a + 1, i + b])
                    if parts:
                        weights[c] = jnp.exp2(scale[z, i] * sum(parts[1:], parts[0]))
                    else:
                        weights[c] = jnp.ones((SUBS, LANES), jnp.float32)
                t = top[z - begin, i]
                s = total[z - begin, i]
                for c in group:
                    t = jnp.maximum(t, weights[c])
                    s = s + weights[c]
                top[z - begin, i] = t
                total[z - begin, i] = s
                if 0 <= z + a < depth:
                    w = weighted[z - begin, i]
                    for c in group:
                        w = w + weights[c] * vals[c + 1, z + a, i + b + 1]
                    weighted[z - begin, i] = w

    for a in range(-2, 3):

        def one(n, _, a=a):
            b = n + jnp.where(n >= 2, 1, 0) if a == 0 else n
            offsets(a, b, range(5))
            return 0

        lax.fori_loop(0, 4 if a == 0 else 5, one, 0)
    offsets(0, 2, (0, 1, 3, 4))

    for z in range(end - begin):
        for i in range(blocks):
            t = top[z, i]
            out[z, pl.ds(i, SUBS, stride=blocks), :] = (
                weighted[z, i] + t * vals[3, z + begin, i + 3]
            ) / (total[z, i] + t)


def denoise(volume, strength):
    depth, size_x, size_y = strength.shape
    sizes = {axis: lax.axis_size(axis) for axis in ("gx", "gy", "off")}
    gxs, gys, offs = sizes["gx"], sizes["gy"], sizes["off"]
    rows = size_x // offs
    blocks = rows // SUBS
    tall = rows + 2 * SUBS
    assert size_y == LANES and offs > 1
    tile = (SUBS, LANES)
    f32 = jnp.float32
    strips, corner, layer = pl.pallas_call(
        pack_kernel(rows),
        out_shape=[
            jax.ShapeDtypeStruct((tall, LANES), f32),
            jax.ShapeDtypeStruct(tile, f32),
            jax.ShapeDtypeStruct((depth,) + tile, f32),
        ],
        in_specs=[VMEM],
        out_specs=[VMEM] * 3,
    )(volume)

    def across(swap):
        moves = []
        for x in range(gxs):
            for y in range(gys):
                for k in range(offs):
                    to = (x + (1 if k == 0 else -1)) % gxs
                    moves.append(((x * gys + y) * offs + k, (to * gys + swap[y]) * offs + k))
        return moves

    axes = ("gx", "gy", "off")
    first, second = partners(gys)
    near = lax.ppermute(strips, "gy", list(enumerate(first)))
    far = lax.ppermute(strips, "gy", list(enumerate(second)))
    layer = lax.ppermute(layer, axes, across(list(range(gys))))
    near_corner = lax.ppermute(corner, axes, across(first))
    far_corner = lax.ppermute(corner, axes, across(second))
    half = depth // 2
    limit = 16 * 2**20
    prepared = [
        jax.ShapeDtypeStruct((7, depth, blocks + 6) + tile, f32),
        jax.ShapeDtypeStruct((3, depth, blocks + 2) + tile, f32),
        jax.ShapeDtypeStruct((5, depth + 2, blocks + 4) + tile, f32),
        jax.ShapeDtypeStruct((depth, blocks) + tile, f32),
    ]

    def sums(slices):
        return [pltpu.VMEM((slices, blocks) + tile, f32)] * 3

    head, *prepared = pl.pallas_call(
        prepare_kernel(depth, rows, blocks, (0, half)),
        out_shape=[jax.ShapeDtypeStruct((half, rows, size_y), f32)] + prepared,
        in_specs=[VMEM, pl.BlockSpec(memory_space=pl.ANY)] + [VMEM] * 5,
        out_specs=[VMEM] * 5,
        scratch_shapes=[
            pltpu.VMEM((7, tall, LANES), f32),
            pltpu.VMEM((depth, rows, LANES), f32),
            pltpu.SemaphoreType.DMA,
        ]
        + sums(half),
        compiler_params=pltpu.CompilerParams(vmem_limit_bytes=limit),
    )(volume, strength, layer, near, far, near_corner, far_corner)

    def second_kernel(vals, cent, energy, scale, out, *sums):
        weigh(depth, blocks, (half, depth), vals, cent, energy, scale, out, *sums)

    work = 124 * 20 * (depth - half) * rows * size_y
    tail = pl.pallas_call(
        second_kernel,
        out_shape=jax.ShapeDtypeStruct((depth - half, rows, size_y), f32),
        in_specs=[VMEM] * 4,
        out_specs=VMEM,
        scratch_shapes=sums(depth - half),
        compiler_params=pltpu.CompilerParams(vmem_limit_bytes=limit),
        cost_estimate=pl.CostEstimate(flops=work, bytes_accessed=work // 2, transcendentals=0),
    )(*prepared)
    return head, tail


def gathered(parts):
    count = lax.axis_size("off")
    off = lax.axis_index("off")
    rows, size_y = parts[0].shape[1:]
    depth = sum(part.shape[0] for part in parts)
    whole = jnp.zeros((count, depth, rows, size_y), parts[0].dtype)
    z = 0
    for part in parts:
        whole = lax.dynamic_update_slice(whole, part[None], (off, z, 0, 0))
        for step in range(1, count):
            moves = [(i, i ^ step) for i in range(count)]
            other = lax.ppermute(part, "off", moves)
            whole = lax.dynamic_update_slice(whole, other[None], (off ^ step, z, 0, 0))
        z += part.shape[0]
    return jnp.swapaxes(whole, 0, 1).reshape(depth, count * rows, size_y)


def shards(volume, strength):
    return gathered(denoise(volume, strength))


def solution(mesh):
    return jax.shard_map(
        shards,
        mesh=mesh,
        in_specs=(P(None, "gx", "gy"), P(None, "gx", "gy")),
        out_specs=P(None, "gx", "gy"),
        check_vma=False,
    )
```

```python
import math

import jax
import jax.numpy as jnp
from jax import lax
from jax.experimental import pallas as pl
from jax.experimental.pallas import tpu as pltpu
from jax.sharding import PartitionSpec as P

EDGE = math.exp(-0.5) / (1.0 + 2.0 * math.exp(-0.5))
GAIN = math.exp(0.5)
SCALE = -(EDGE**3) * math.log2(math.e)
LANES = 128
SUBS = 8
VMEM = pl.BlockSpec(memory_space=pltpu.VMEM)


def partners(count):
    assert count % 2 == 0
    first = [i ^ 1 for i in range(count)]
    second = [(((i + 1) ^ 1) - 1) % count for i in range(count)]
    return first, second


def packed(slices, lane):
    place = (lane + 3) % LANES
    line = jnp.zeros((SUBS, LANES), jnp.float32)
    for z, v in enumerate(slices):
        v = pltpu.roll(v, 16 * z, 1) if z else v
        line = jnp.where((place >= 16 * z) & (place < 16 * z + 6), v, line)
    return line


def lanes():
    return lax.broadcasted_iota(jnp.int32, (SUBS, LANES), 1)


def layer_kernel(volume, layer, arrived):
    off, size_x = lax.axis_index("off"), volume.shape[1]
    at = pl.multiple_of(jnp.where(off == 0, size_x - SUBS, 0), SUBS)
    copy = pltpu.make_async_copy(volume.at[:, pl.ds(at, SUBS), :], layer, arrived)
    copy.start()
    copy.wait()


def window(off, rows, size_x):
    begin = pl.multiple_of(jnp.clip(off * rows - SUBS, 0, size_x - rows - 2 * SUBS), SUBS)

    def block(j):
        at = jnp.clip(off * rows + SUBS * (j - 1), 0, size_x - SUBS) - begin
        return pl.ds(pl.multiple_of(at, SUBS), SUBS)

    return begin, block


def pack_kernel(rows, size_x):
    blocks = rows // SUBS

    def kernel(volume, strength, strips, mine, scale, local, arrived):
        depth = volume.shape[0]
        off = lax.axis_index("off")
        begin, block = window(off, rows, size_x)
        first = pltpu.make_async_copy(
            volume.at[:, pl.ds(begin, rows + 2 * SUBS), :], mine, arrived.at[0]
        )
        start = pl.multiple_of(off * rows, SUBS)
        second = pltpu.make_async_copy(
            strength.at[:, pl.ds(start, rows), :], local, arrived.at[1]
        )
        first.start()
        second.start()
        lane = lanes()
        first.wait()
        for j in range(blocks + 2):
            strips[pl.ds(SUBS * j, SUBS), :] = packed(
                [mine[z, block(j), :] for z in range(depth)], lane
            )
        second.wait()
        for z in range(depth):
            for i in range(blocks):
                scale[z, i] = SCALE / local[z, pl.ds(i, SUBS, stride=blocks), :]

    return kernel


def edges(tall):
    off, offs = lax.axis_index("off"), lax.axis_size("off")
    gx, gxs = lax.axis_index("gx"), lax.axis_size("gx")
    return {0: (off == 0, gx == 0), tall - 1: (off == offs - 1, gx == gxs - 1)}


def join_kernel(strips, layer, joined):
    depth, tall = layer.shape[0], strips.shape[0] // SUBS
    line = packed([layer[z] for z in range(depth)], lanes())
    for j in range(tall):
        at = pl.ds(SUBS * j, SUBS)
        value = strips[at, :]
        for end, (outside, beyond) in edges(tall).items():
            if j == end:
                value = jnp.where(outside, jnp.where(beyond, 0.0, line), value)
        joined[at, :] = value


def three(a, b, c):
    return a + c + GAIN * b


def main_kernel(depth, rows, blocks, size_x):
    wide = blocks + 6
    tall = rows // SUBS + 2

    def kernel(mine, scale, layer, near, far, out, flat, vals, cent, energy, *sums):
        lane = lanes()
        _, block = window(lax.axis_index("off"), rows, size_x)
        gy, gys = lax.axis_index("gy"), lax.axis_size("gy")
        outer = lane % 16 >= 13
        closed = (outer & (gy == 0)) | ((lane % 16 < 3) & (gy == gys - 1))
        from_near = outer == (gy % 2 == 1)
        ends = edges(tall)

        def side(j):
            at = pl.ds(SUBS * j, SUBS)
            return jnp.where(closed, 0.0, jnp.where(from_near, near[at, :], far[at, :]))

        lines = [side(j) for j in range(tall)]

        def fill(z):
            for r in range(tall):
                at = pl.ds(SUBS * r, SUBS)
                v = mine[z, block(r), :]
                if r in ends:
                    v = jnp.where(ends[r][0], jnp.where(ends[r][1], 0.0, layer[z]), v)
                h = pltpu.roll(lines[r], LANES - 16 * z, 1)
                flat[3, at, :] = v
                for c in range(1, 4):
                    flat[3 + c, at, :] = pltpu.roll(jnp.where(lane < c, h, v), LANES - c, 1)
                    flat[3 - c, at, :] = pltpu.roll(jnp.where(lane >= LANES - c, h, v), c, 1)
            for i in range(wide):
                for c in range(7):
                    v = flat[c, pl.ds(SUBS - 3 + i, SUBS, stride=blocks), :]
                    vals[c, z, i] = v
                    if 2 <= c <= 4 and 2 <= i < wide - 2:
                        cent[c - 2, z, i - 2] = (-2.0 * GAIN if c == 3 else -2.0) * v

        for z in range(depth):
            fill(z)

        def energies(c, _):
            count = blocks + 4
            filtered = []

            def store(z):
                for i in range(count):
                    e = GAIN * filtered[z][i] if 0 <= z < depth else None
                    for y in (z - 1, z + 1):
                        if 0 <= y < depth:
                            e = filtered[y][i] if e is None else e + filtered[y][i]
                    energy[c, z + 1, i] = e

            for z in range(depth):
                line = []
                for i in range(wide):
                    u, v, w = (vals[c + k, z, i] for k in range(3))
                    line.append(three(u * u, v * v, w * w))
                filtered.append([three(*line[i : i + 3]) for i in range(count)])
                store(z - 1)
            store(depth - 1)
            store(depth)
            return 0

        lax.fori_loop(0, 5, energies, 0)

        weigh(depth, blocks, vals, cent, energy, scale, out, *sums)

    return kernel


def weigh(depth, blocks, vals, cent, energy, scale, out, top, total, weighted):
    begin, end = 0, depth
    for z in range(end - begin):
        for i in range(blocks):
            for ref in (top, total, weighted):
                ref[z, i] = jnp.zeros((SUBS, LANES), jnp.float32)

    def offsets(a, b, group):
        first, last = max(0, -a, begin - 1), min(depth, depth - a, end + 1)
        planes = sorted({c + k for c in group for k in range(3)})
        filtered = {}

        def emit(z):
            if not first <= z < last:
                return
            lines = {c: [] for c in group}
            for i in range(blocks + 2):
                v = {k: vals[k, z + a, i + b] for k in planes}
                m = [cent[k, z, i] for k in range(3)]
                for c in group:
                    lines[c].append(m[0] * v[c] + m[2] * v[c + 2] + m[1] * v[c + 1])
            filtered[z] = {
                c: [three(*lines[c][i : i + 3]) for i in range(blocks)] for c in group
            }

        emit(begin - 1)
        emit(begin)
        for z in range(begin, end):
            emit(z + 1)
            for i in range(blocks):
                weights = {}
                for c in group:
                    parts = [filtered[y][c][i] for y in (z - 1, z + 1) if y in filtered]
                    if z in filtered:
                        parts.append(GAIN * filtered[z][c][i])
                    if -1 <= z + a <= depth:
                        parts.append(energy[c, z + a + 1, i + b])
                    if parts:
                        weights[c] = jnp.exp2(scale[z, i] * sum(parts[1:], parts[0]))
                    else:
                        weights[c] = jnp.ones((SUBS, LANES), jnp.float32)
                t = top[z - begin, i]
                s = total[z - begin, i]
                for c in group:
                    t = jnp.maximum(t, weights[c])
                    s = s + weights[c]
                top[z - begin, i] = t
                total[z - begin, i] = s
                if 0 <= z + a < depth:
                    w = weighted[z - begin, i]
                    for c in group:
                        w = w + weights[c] * vals[c + 1, z + a, i + b + 1]
                    weighted[z - begin, i] = w

    for a in range(-2, 3):

        def one(n, _, a=a):
            b = n + jnp.where(n >= 2, 1, 0) if a == 0 else n
            offsets(a, b, range(5))
            return 0

        lax.fori_loop(0, 4 if a == 0 else 5, one, 0)
    offsets(0, 2, (0, 1, 3, 4))

    for z in range(end - begin):
        for i in range(blocks):
            t = top[z, i]
            out[z, pl.ds(i, SUBS, stride=blocks), :] = (
                weighted[z, i] + t * vals[3, z + begin, i + 3]
            ) / (total[z, i] + t)


def place_kernel(part, off, *refs):
    *_, out, done = refs
    rows = part.shape[1]
    at = pl.ds(pl.multiple_of(off[0] * rows, SUBS), rows)
    copy = pltpu.make_async_copy(part, out.at[:, at, :], done)
    copy.start()
    copy.wait()


def shards(volume, strength):
    depth, size_x, size_y = strength.shape
    gxs, gys, offs = (lax.axis_size(axis) for axis in ("gx", "gy", "off"))
    rows = size_x // offs
    blocks = rows // SUBS
    tall = rows + 2 * SUBS
    assert size_y == LANES and offs > 1
    tile = (SUBS, LANES)
    f32 = jnp.float32
    HBM = pl.BlockSpec(memory_space=pltpu.HBM)

    small = pltpu.CompilerParams(vmem_limit_bytes=4 * 2**20)

    def shape(*sizes):
        return jax.ShapeDtypeStruct(sizes, f32)

    layer = pl.pallas_call(
        layer_kernel,
        out_shape=shape(depth, *tile),
        in_specs=[HBM],
        out_specs=VMEM,
        scratch_shapes=[pltpu.SemaphoreType.DMA],
    )(volume)
    moves = []
    for x in range(gxs):
        for k in range(offs):
            to = (x + (1 if k == 0 else -1)) % gxs
            moves.append((x * offs + k, to * offs + k))
    layer = lax.ppermute(layer, ("gx", "off"), moves)
    strips, mine, scale = pl.pallas_call(
        pack_kernel(rows, size_x),
        out_shape=[shape(tall, LANES), shape(depth, tall, LANES), shape(depth, blocks, *tile)],
        in_specs=[HBM, HBM],
        out_specs=[VMEM] * 3,
        scratch_shapes=[pltpu.VMEM((depth, rows, LANES), f32), pltpu.SemaphoreType.DMA((2,))],
        cost_estimate=pl.CostEstimate(flops=4_000_000, bytes_accessed=4_000_000, transcendentals=0),
        compiler_params=small,
    )(volume, strength)
    strips = pl.pallas_call(
        join_kernel,
        out_shape=shape(tall, LANES),
        in_specs=[VMEM] * 2,
        out_specs=VMEM,
        compiler_params=small,
    )(strips, layer)
    first, second = partners(gys)
    near = lax.ppermute(strips, "gy", list(enumerate(first)))
    far = lax.ppermute(strips, "gy", list(enumerate(second)))
    part = pl.pallas_call(
        main_kernel(depth, rows, blocks, size_x),
        out_shape=shape(depth, rows, size_y),
        in_specs=[VMEM] * 5,
        out_specs=VMEM,
        scratch_shapes=[
            pltpu.VMEM((7, tall, LANES), f32),
            pltpu.VMEM((7, depth, blocks + 6) + tile, f32),
            pltpu.VMEM((3, depth, blocks + 2) + tile, f32),
            pltpu.VMEM((5, depth + 2, blocks + 4) + tile, f32),
        ]
        + [pltpu.VMEM((depth, blocks) + tile, f32)] * 3,
        compiler_params=pltpu.CompilerParams(vmem_limit_bytes=16 * 2**20),
    )(mine, scale, layer, near, far)

    off = lax.axis_index("off")
    SMEM = pl.BlockSpec(memory_space=pltpu.SMEM)

    def place(block, source, whole):
        held = [] if whole is None else [whole]
        return pl.pallas_call(
            place_kernel,
            out_shape=shape(depth, size_x, size_y),
            in_specs=[VMEM, SMEM] + [HBM] * len(held),
            out_specs=HBM,
            scratch_shapes=[pltpu.SemaphoreType.DMA],
            input_output_aliases={2: 0} if held else {},
            compiler_params=small,
        )(block, source[None].astype(jnp.int32), *held)

    whole = place(part, off, None)
    for step in range(1, offs):
        other = lax.ppermute(part, "off", [(i, i ^ step) for i in range(offs)])
        whole = place(other, off ^ step, whole)
    return whole


def solution(mesh):
    return jax.shard_map(
        shards,
        mesh=mesh,
        in_specs=(P(None, "gx", "gy"), P(None, "gx", "gy")),
        out_specs=P(None, "gx", "gy"),
        check_vma=False,
    )
```

```python
import math

import jax
import jax.numpy as jnp
from jax import lax
from jax.experimental import pallas as pl
from jax.experimental.pallas import tpu as pltpu
from jax.sharding import PartitionSpec as P

EDGE = math.exp(-0.5) / (1.0 + 2.0 * math.exp(-0.5))
GAIN = math.exp(0.5)
SCALE = -(EDGE**3) * math.log2(math.e)
LANES = 128
SUBS = 8
VMEM = pl.BlockSpec(memory_space=pltpu.VMEM)


def partners(count):
    assert count % 2 == 0
    first = [i ^ 1 for i in range(count)]
    second = [(((i + 1) ^ 1) - 1) % count for i in range(count)]
    return first, second


def packed(slices, lane):
    place = (lane + 3) % LANES
    line = jnp.zeros((SUBS, LANES), jnp.float32)
    for z, v in enumerate(slices):
        v = pltpu.roll(v, 16 * z, 1) if z else v
        line = jnp.where((place >= 16 * z) & (place < 16 * z + 6), v, line)
    return line


def lanes():
    return lax.broadcasted_iota(jnp.int32, (SUBS, LANES), 1)


def layer_kernel(volume, layer, arrived):
    off, size_x = lax.axis_index("off"), volume.shape[1]
    at = pl.multiple_of(jnp.where(off == 0, size_x - SUBS, 0), SUBS)
    copy = pltpu.make_async_copy(volume.at[:, pl.ds(at, SUBS), :], layer, arrived)
    copy.start()
    copy.wait()


def window(off, rows, size_x):
    begin = pl.multiple_of(jnp.clip(off * rows - SUBS, 0, size_x - rows - 2 * SUBS), SUBS)

    def block(j):
        at = jnp.clip(off * rows + SUBS * (j - 1), 0, size_x - SUBS) - begin
        return pl.ds(pl.multiple_of(at, SUBS), SUBS)

    return begin, block


def pack_kernel(rows, size_x):
    blocks = rows // SUBS

    def kernel(volume, strength, strips, mine, scale, local, arrived):
        depth = volume.shape[0]
        off = lax.axis_index("off")
        begin, block = window(off, rows, size_x)
        first = pltpu.make_async_copy(
            volume.at[:, pl.ds(begin, rows + 2 * SUBS), :], mine, arrived.at[0]
        )
        start = pl.multiple_of(off * rows, SUBS)
        second = pltpu.make_async_copy(
            strength.at[:, pl.ds(start, rows), :], local, arrived.at[1]
        )
        first.start()
        second.start()
        lane = lanes()
        first.wait()
        for j in range(blocks + 2):
            strips[pl.ds(SUBS * j, SUBS), :] = packed(
                [mine[z, block(j), :] for z in range(depth)], lane
            )
        second.wait()
        for z in range(depth):
            for i in range(blocks):
                scale[z, i] = SCALE / local[z, pl.ds(i, SUBS, stride=blocks), :]

    return kernel


def edges(tall):
    off, offs = lax.axis_index("off"), lax.axis_size("off")
    gx, gxs = lax.axis_index("gx"), lax.axis_size("gx")
    return {0: (off == 0, gx == 0), tall - 1: (off == offs - 1, gx == gxs - 1)}


def join_kernel(strips, layer, joined):
    depth, tall = layer.shape[0], strips.shape[0] // SUBS
    line = packed([layer[z] for z in range(depth)], lanes())
    for j in range(tall):
        at = pl.ds(SUBS * j, SUBS)
        value = strips[at, :]
        for end, (outside, beyond) in edges(tall).items():
            if j == end:
                value = jnp.where(outside, jnp.where(beyond, 0.0, line), value)
        joined[at, :] = value


def three(a, b, c):
    return a + c + GAIN * b


def main_kernel(depth, rows, blocks, size_x):
    wide = blocks + 6
    tall = rows // SUBS + 2

    def kernel(mine, scale, layer, near, far, out, flat, vals, cent, energy, *sums):
        lane = lanes()
        _, block = window(lax.axis_index("off"), rows, size_x)
        gy, gys = lax.axis_index("gy"), lax.axis_size("gy")
        outer = lane % 16 >= 13
        closed = (outer & (gy == 0)) | ((lane % 16 < 3) & (gy == gys - 1))
        from_near = outer == (gy % 2 == 1)
        ends = edges(tall)

        def side(j):
            at = pl.ds(SUBS * j, SUBS)
            return jnp.where(closed, 0.0, jnp.where(from_near, near[at, :], far[at, :]))

        lines = [side(j) for j in range(tall)]

        def fill(z):
            for r in range(tall):
                at = pl.ds(SUBS * r, SUBS)
                v = mine[z, block(r), :]
                if r in ends:
                    v = jnp.where(ends[r][0], jnp.where(ends[r][1], 0.0, layer[z]), v)
                h = pltpu.roll(lines[r], LANES - 16 * z, 1)
                flat[3, at, :] = v
                for c in range(1, 4):
                    flat[3 + c, at, :] = pltpu.roll(jnp.where(lane < c, h, v), LANES - c, 1)
                    flat[3 - c, at, :] = pltpu.roll(jnp.where(lane >= LANES - c, h, v), c, 1)
            for i in range(wide):
                for c in range(7):
                    v = flat[c, pl.ds(SUBS - 3 + i, SUBS, stride=blocks), :]
                    vals[c, z, i] = v
                    if 2 <= c <= 4 and 2 <= i < wide - 2:
                        cent[c - 2, z, i - 2] = (-2.0 * GAIN if c == 3 else -2.0) * v

        for z in range(depth):
            fill(z)

        def energies(c, _):
            count = blocks + 4
            filtered = []

            def store(z):
                for i in range(count):
                    e = GAIN * filtered[z][i] if 0 <= z < depth else None
                    for y in (z - 1, z + 1):
                        if 0 <= y < depth:
                            e = filtered[y][i] if e is None else e + filtered[y][i]
                    energy[c, z + 1, i] = e

            for z in range(depth):
                line = []
                for i in range(wide):
                    u, v, w = (vals[c + k, z, i] for k in range(3))
                    line.append(three(u * u, v * v, w * w))
                filtered.append([three(*line[i : i + 3]) for i in range(count)])
                store(z - 1)
            store(depth - 1)
            store(depth)
            return 0

        lax.fori_loop(0, 5, energies, 0)

        weigh(depth, blocks, vals, cent, energy, scale, out, *sums)

    return kernel


def weigh(depth, blocks, vals, cent, energy, scale, out, top, total, weighted):
    begin, end = 0, depth
    for z in range(end - begin):
        for i in range(blocks):
            for ref in (top, total, weighted):
                ref[z, i] = jnp.zeros((SUBS, LANES), jnp.float32)

    def offsets(a, b, group):
        first, last = max(0, -a, begin - 1), min(depth, depth - a, end + 1)
        planes = sorted({c + k for c in group for k in range(3)})
        filtered = {}

        def emit(z):
            if not first <= z < last:
                return
            lines = {c: [] for c in group}
            for i in range(blocks + 2):
                v = {k: vals[k, z + a, i + b] for k in planes}
                m = [cent[k, z, i] for k in range(3)]
                for c in group:
                    lines[c].append(m[0] * v[c] + m[2] * v[c + 2] + m[1] * v[c + 1])
            filtered[z] = {
                c: [three(*lines[c][i : i + 3]) for i in range(blocks)] for c in group
            }

        emit(begin - 1)
        emit(begin)
        for z in range(begin, end):
            emit(z + 1)
            for i in range(blocks):
                weights = {}
                for c in group:
                    parts = [filtered[y][c][i] for y in (z - 1, z + 1) if y in filtered]
                    if z in filtered:
                        parts.append(GAIN * filtered[z][c][i])
                    if -1 <= z + a <= depth:
                        parts.append(energy[c, z + a + 1, i + b])
                    if parts:
                        weights[c] = jnp.exp2(scale[z, i] * sum(parts[1:], parts[0]))
                    else:
                        weights[c] = jnp.ones((SUBS, LANES), jnp.float32)
                t = top[z - begin, i]
                s = total[z - begin, i]
                for c in group:
                    t = jnp.maximum(t, weights[c])
                    s = s + weights[c]
                top[z - begin, i] = t
                total[z - begin, i] = s
                if 0 <= z + a < depth:
                    w = weighted[z - begin, i]
                    for c in group:
                        w = w + weights[c] * vals[c + 1, z + a, i + b + 1]
                    weighted[z - begin, i] = w

    for a in range(-2, 3):

        def one(n, _, a=a):
            b = n + jnp.where(n >= 2, 1, 0) if a == 0 else n
            offsets(a, b, range(5))
            return 0

        lax.fori_loop(0, 4 if a == 0 else 5, one, 0)
    offsets(0, 2, (0, 1, 3, 4))

    for z in range(end - begin):
        for i in range(blocks):
            t = top[z, i]
            out[z, pl.ds(i, SUBS, stride=blocks), :] = (
                weighted[z, i] + t * vals[3, z + begin, i + 3]
            ) / (total[z, i] + t)


def place_kernel(count, rows):
    def kernel(*refs):
        parts, sources, (*_, out, done) = refs[:count], refs[count], refs[count + 1 :]
        copies = []
        for n, part in enumerate(parts):
            at = pl.ds(pl.multiple_of(sources[n] * rows, SUBS), rows)
            copies.append(pltpu.make_async_copy(part, out.at[:, at, :], done.at[n]))
            copies[n].start()
        for copy in copies:
            copy.wait()

    return kernel


def shards(volume, strength):
    depth, size_x, size_y = strength.shape
    gxs, gys, offs = (lax.axis_size(axis) for axis in ("gx", "gy", "off"))
    rows = size_x // offs
    blocks = rows // SUBS
    tall = rows + 2 * SUBS
    assert size_y == LANES and offs > 1
    tile = (SUBS, LANES)
    f32 = jnp.float32
    HBM = pl.BlockSpec(memory_space=pltpu.HBM)

    small = pltpu.CompilerParams(vmem_limit_bytes=4 * 2**20)

    def shape(*sizes):
        return jax.ShapeDtypeStruct(sizes, f32)

    layer = pl.pallas_call(
        layer_kernel,
        out_shape=shape(depth, *tile),
        in_specs=[HBM],
        out_specs=VMEM,
        scratch_shapes=[pltpu.SemaphoreType.DMA],
        compiler_params=small,
    )(volume)
    moves = []
    for x in range(gxs):
        for k in range(offs):
            to = (x + (1 if k == 0 else -1)) % gxs
            moves.append((x * offs + k, to * offs + k))
    layer = lax.ppermute(layer, ("gx", "off"), moves)
    strips, mine, scale = pl.pallas_call(
        pack_kernel(rows, size_x),
        out_shape=[shape(tall, LANES), shape(depth, tall, LANES), shape(depth, blocks, *tile)],
        in_specs=[HBM, HBM],
        out_specs=[VMEM] * 3,
        scratch_shapes=[pltpu.VMEM((depth, rows, LANES), f32), pltpu.SemaphoreType.DMA((2,))],
        cost_estimate=pl.CostEstimate(flops=4_000_000, bytes_accessed=4_000_000, transcendentals=0),
        compiler_params=small,
    )(volume, strength)
    strips = pl.pallas_call(
        join_kernel,
        out_shape=shape(tall, LANES),
        in_specs=[VMEM] * 2,
        out_specs=VMEM,
        compiler_params=small,
    )(strips, layer)
    first, second = partners(gys)
    near = lax.ppermute(strips, "gy", list(enumerate(first)))
    far = lax.ppermute(strips, "gy", list(enumerate(second)))
    part = pl.pallas_call(
        main_kernel(depth, rows, blocks, size_x),
        out_shape=shape(depth, rows, size_y),
        in_specs=[VMEM] * 5,
        out_specs=VMEM,
        scratch_shapes=[
            pltpu.VMEM((7, tall, LANES), f32),
            pltpu.VMEM((7, depth, blocks + 6) + tile, f32),
            pltpu.VMEM((3, depth, blocks + 2) + tile, f32),
            pltpu.VMEM((5, depth + 2, blocks + 4) + tile, f32),
        ]
        + [pltpu.VMEM((depth, blocks) + tile, f32)] * 3,
        compiler_params=pltpu.CompilerParams(vmem_limit_bytes=16 * 2**20),
    )(mine, scale, layer, near, far)

    off = lax.axis_index("off")
    SMEM = pl.BlockSpec(memory_space=pltpu.SMEM)

    def place(blocks, whole):
        count = len(blocks)
        held = [] if whole is None else [whole]
        sources = jnp.stack([off ^ step for step, _ in blocks]).astype(jnp.int32)
        return pl.pallas_call(
            place_kernel(count, rows),
            out_shape=shape(depth, size_x, size_y),
            in_specs=[VMEM] * count + [SMEM] + [HBM] * len(held),
            out_specs=HBM,
            scratch_shapes=[pltpu.SemaphoreType.DMA((count,))],
            input_output_aliases={count + 1: 0} if held else {},
            compiler_params=small,
        )(*(block for _, block in blocks), sources, *held)

    assert offs & (offs - 1) == 0
    blocks, bit = [(0, part)], offs // 2
    while bit:
        swap = [(i, i ^ bit) for i in range(offs)]
        blocks += [(step ^ bit, lax.ppermute(block, "off", swap)) for step, block in blocks]
        bit //= 2
    return place(blocks[-1:], place(blocks[:-1], None))


def solution(mesh):
    return jax.shard_map(
        shards,
        mesh=mesh,
        in_specs=(P(None, "gx", "gy"), P(None, "gx", "gy")),
        out_specs=P(None, "gx", "gy"),
        check_vma=False,
    )
```

```python
import math

import jax
import jax.numpy as jnp
from jax import lax
from jax.experimental import pallas as pl
from jax.experimental.pallas import tpu as pltpu
from jax.sharding import PartitionSpec as P

EDGE = math.exp(-0.5) / (1.0 + 2.0 * math.exp(-0.5))
GAIN = math.exp(0.5)
SCALE = -(EDGE**3) * math.log2(math.e)
LANES = 128
SUBS = 8
VMEM = pl.BlockSpec(memory_space=pltpu.VMEM)


def partners(count):
    assert count % 2 == 0
    first = [i ^ 1 for i in range(count)]
    second = [(((i + 1) ^ 1) - 1) % count for i in range(count)]
    return first, second


def packed(slices, lane):
    place = (lane + 3) % LANES
    line = jnp.zeros((SUBS, LANES), jnp.float32)
    for z, v in enumerate(slices):
        v = pltpu.roll(v, 16 * z, 1) if z else v
        line = jnp.where((place >= 16 * z) & (place < 16 * z + 6), v, line)
    return line


def lanes():
    return lax.broadcasted_iota(jnp.int32, (SUBS, LANES), 1)


def layer_kernel(volume, layer, arrived):
    off, size_x = lax.axis_index("off"), volume.shape[1]
    at = pl.multiple_of(jnp.where(off == 0, size_x - SUBS, 0), SUBS)
    copy = pltpu.make_async_copy(volume.at[:, pl.ds(at, SUBS), :], layer, arrived)
    copy.start()
    copy.wait()


def window(off, rows, size_x):
    begin = pl.multiple_of(jnp.clip(off * rows - SUBS, 0, size_x - rows - 2 * SUBS), SUBS)

    def block(j):
        at = jnp.clip(off * rows + SUBS * (j - 1), 0, size_x - SUBS) - begin
        return pl.ds(pl.multiple_of(at, SUBS), SUBS)

    return begin, block


def pack_kernel(rows, size_x):
    blocks = rows // SUBS

    def kernel(volume, strength, strips, mine, scale, local, arrived):
        depth = volume.shape[0]
        off = lax.axis_index("off")
        begin, block = window(off, rows, size_x)
        first = pltpu.make_async_copy(
            volume.at[:, pl.ds(begin, rows + 2 * SUBS), :], mine, arrived.at[0]
        )
        start = pl.multiple_of(off * rows, SUBS)
        second = pltpu.make_async_copy(
            strength.at[:, pl.ds(start, rows), :], local, arrived.at[1]
        )
        first.start()
        second.start()
        lane = lanes()
        first.wait()
        for j in range(blocks + 2):
            strips[pl.ds(SUBS * j, SUBS), :] = packed(
                [mine[z, block(j), :] for z in range(depth)], lane
            )
        second.wait()
        for z in range(depth):
            for i in range(blocks):
                scale[z, i] = SCALE / local[z, pl.ds(i, SUBS, stride=blocks), :]

    return kernel


def edges(tall):
    off, offs = lax.axis_index("off"), lax.axis_size("off")
    gx, gxs = lax.axis_index("gx"), lax.axis_size("gx")
    return {0: (off == 0, gx == 0), tall - 1: (off == offs - 1, gx == gxs - 1)}


def join_kernel(strips, layer, joined):
    depth, tall = layer.shape[0], strips.shape[0] // SUBS
    line = packed([layer[z] for z in range(depth)], lanes())
    for j in range(tall):
        at = pl.ds(SUBS * j, SUBS)
        value = strips[at, :]
        for end, (outside, beyond) in edges(tall).items():
            if j == end:
                value = jnp.where(outside, jnp.where(beyond, 0.0, line), value)
        joined[at, :] = value


def three(a, b, c):
    return a + c + GAIN * b


def main_kernel(depth, rows, blocks, size_x):
    wide = blocks + 6
    tall = rows // SUBS + 2

    def kernel(mine, scale, layer, near, far, out, low, high, flat, vals, cent, energy, *sums):
        lane = lanes()
        _, block = window(lax.axis_index("off"), rows, size_x)
        gy, gys = lax.axis_index("gy"), lax.axis_size("gy")
        outer = lane % 16 >= 13
        closed = (outer & (gy == 0)) | ((lane % 16 < 3) & (gy == gys - 1))
        from_near = outer == (gy % 2 == 1)
        ends = edges(tall)

        def side(j):
            at = pl.ds(SUBS * j, SUBS)
            return jnp.where(closed, 0.0, jnp.where(from_near, near[at, :], far[at, :]))

        lines = [side(j) for j in range(tall)]

        def fill(z):
            for r in range(tall):
                at = pl.ds(SUBS * r, SUBS)
                v = mine[z, block(r), :]
                if r in ends:
                    v = jnp.where(ends[r][0], jnp.where(ends[r][1], 0.0, layer[z]), v)
                h = pltpu.roll(lines[r], LANES - 16 * z, 1)
                flat[3, at, :] = v
                for c in range(1, 4):
                    flat[3 + c, at, :] = pltpu.roll(jnp.where(lane < c, h, v), LANES - c, 1)
                    flat[3 - c, at, :] = pltpu.roll(jnp.where(lane >= LANES - c, h, v), c, 1)
            for i in range(wide):
                for c in range(7):
                    v = flat[c, pl.ds(SUBS - 3 + i, SUBS, stride=blocks), :]
                    vals[c, z, i] = v
                    if 2 <= c <= 4 and 2 <= i < wide - 2:
                        cent[c - 2, z, i - 2] = (-2.0 * GAIN if c == 3 else -2.0) * v

        for z in range(depth):
            fill(z)

        def energies(c, _):
            count = blocks + 4
            filtered = []

            def store(z):
                for i in range(count):
                    e = GAIN * filtered[z][i] if 0 <= z < depth else None
                    for y in (z - 1, z + 1):
                        if 0 <= y < depth:
                            e = filtered[y][i] if e is None else e + filtered[y][i]
                    energy[c, z + 1, i] = e

            for z in range(depth):
                line = []
                for i in range(wide):
                    u, v, w = (vals[c + k, z, i] for k in range(3))
                    line.append(three(u * u, v * v, w * w))
                filtered.append([three(*line[i : i + 3]) for i in range(count)])
                store(z - 1)
            store(depth - 1)
            store(depth)
            return 0

        lax.fori_loop(0, 5, energies, 0)

        weigh(depth, blocks, vals, cent, energy, scale, (out, low, high), *sums)

    return kernel


def weigh(depth, blocks, vals, cent, energy, scale, outs, top, total, weighted):
    begin, end = 0, depth
    for z in range(end - begin):
        for i in range(blocks):
            for ref in (top, total, weighted):
                ref[z, i] = jnp.zeros((SUBS, LANES), jnp.float32)

    def offsets(a, b, group):
        first, last = max(0, -a, begin - 1), min(depth, depth - a, end + 1)
        planes = sorted({c + k for c in group for k in range(3)})
        filtered = {}

        def emit(z):
            if not first <= z < last:
                return
            lines = {c: [] for c in group}
            for i in range(blocks + 2):
                v = {k: vals[k, z + a, i + b] for k in planes}
                m = [cent[k, z, i] for k in range(3)]
                for c in group:
                    lines[c].append(m[0] * v[c] + m[2] * v[c + 2] + m[1] * v[c + 1])
            filtered[z] = {
                c: [three(*lines[c][i : i + 3]) for i in range(blocks)] for c in group
            }

        emit(begin - 1)
        emit(begin)
        for z in range(begin, end):
            emit(z + 1)
            for i in range(blocks):
                weights = {}
                for c in group:
                    parts = [filtered[y][c][i] for y in (z - 1, z + 1) if y in filtered]
                    if z in filtered:
                        parts.append(GAIN * filtered[z][c][i])
                    if -1 <= z + a <= depth:
                        parts.append(energy[c, z + a + 1, i + b])
                    if parts:
                        weights[c] = jnp.exp2(scale[z, i] * sum(parts[1:], parts[0]))
                    else:
                        weights[c] = jnp.ones((SUBS, LANES), jnp.float32)
                t = top[z - begin, i]
                s = total[z - begin, i]
                for c in group:
                    t = jnp.maximum(t, weights[c])
                    s = s + weights[c]
                top[z - begin, i] = t
                total[z - begin, i] = s
                if 0 <= z + a < depth:
                    w = weighted[z - begin, i]
                    for c in group:
                        w = w + weights[c] * vals[c + 1, z + a, i + b + 1]
                    weighted[z - begin, i] = w

    for a in range(-2, 3):

        def one(n, _, a=a):
            b = n + jnp.where(n >= 2, 1, 0) if a == 0 else n
            offsets(a, b, range(5))
            return 0

        lax.fori_loop(0, 4 if a == 0 else 5, one, 0)
    offsets(0, 2, (0, 1, 3, 4))

    for z in range(end - begin):
        for i in range(blocks):
            t = top[z, i]
            value = (weighted[z, i] + t * vals[3, z + begin, i + 3]) / (total[z, i] + t)
            part = outs[1] if z < depth // 2 else outs[2]
            for ref, at in ((outs[0], z), (part, z % (depth // 2))):
                ref[at, pl.ds(i, SUBS, stride=blocks), :] = value


def place_kernel(count, rows):
    def kernel(*refs):
        parts, sources, (*_, out, done) = refs[:count], refs[count], refs[count + 1 :]
        copies = []
        for n, part in enumerate(parts):
            at = pl.ds(pl.multiple_of(sources[n, 0] * rows, SUBS), rows)
            slices = pl.ds(sources[n, 1], part.shape[0])
            copies.append(pltpu.make_async_copy(part, out.at[slices, at, :], done.at[n]))
            copies[n].start()
        for copy in copies:
            copy.wait()

    return kernel


def shards(volume, strength):
    depth, size_x, size_y = strength.shape
    gxs, gys, offs = (lax.axis_size(axis) for axis in ("gx", "gy", "off"))
    rows = size_x // offs
    blocks = rows // SUBS
    tall = rows + 2 * SUBS
    assert size_y == LANES and offs > 1
    tile = (SUBS, LANES)
    f32 = jnp.float32
    HBM = pl.BlockSpec(memory_space=pltpu.HBM)

    small = pltpu.CompilerParams(vmem_limit_bytes=4 * 2**20)

    def shape(*sizes):
        return jax.ShapeDtypeStruct(sizes, f32)

    layer = pl.pallas_call(
        layer_kernel,
        out_shape=shape(depth, *tile),
        in_specs=[HBM],
        out_specs=VMEM,
        scratch_shapes=[pltpu.SemaphoreType.DMA],
        compiler_params=small,
    )(volume)
    moves = []
    for x in range(gxs):
        for k in range(offs):
            to = (x + (1 if k == 0 else -1)) % gxs
            moves.append((x * offs + k, to * offs + k))
    layer = lax.ppermute(layer, ("gx", "off"), moves)
    strips, mine, scale = pl.pallas_call(
        pack_kernel(rows, size_x),
        out_shape=[shape(tall, LANES), shape(depth, tall, LANES), shape(depth, blocks, *tile)],
        in_specs=[HBM, HBM],
        out_specs=[VMEM] * 3,
        scratch_shapes=[pltpu.VMEM((depth, rows, LANES), f32), pltpu.SemaphoreType.DMA((2,))],
        cost_estimate=pl.CostEstimate(flops=4_000_000, bytes_accessed=4_000_000, transcendentals=0),
        compiler_params=small,
    )(volume, strength)
    strips = pl.pallas_call(
        join_kernel,
        out_shape=shape(tall, LANES),
        in_specs=[VMEM] * 2,
        out_specs=VMEM,
        compiler_params=small,
    )(strips, layer)
    first, second = partners(gys)
    near = lax.ppermute(strips, "gy", list(enumerate(first)))
    far = lax.ppermute(strips, "gy", list(enumerate(second)))
    half = depth // 2
    part, *halves = pl.pallas_call(
        main_kernel(depth, rows, blocks, size_x),
        out_shape=[shape(depth, rows, size_y)] + [shape(half, rows, size_y)] * 2,
        in_specs=[VMEM] * 5,
        out_specs=[VMEM] * 3,
        scratch_shapes=[
            pltpu.VMEM((7, tall, LANES), f32),
            pltpu.VMEM((7, depth, blocks + 6) + tile, f32),
            pltpu.VMEM((3, depth, blocks + 2) + tile, f32),
            pltpu.VMEM((5, depth + 2, blocks + 4) + tile, f32),
        ]
        + [pltpu.VMEM((depth, blocks) + tile, f32)] * 3,
        compiler_params=pltpu.CompilerParams(vmem_limit_bytes=16 * 2**20),
    )(mine, scale, layer, near, far)

    off = lax.axis_index("off")
    SMEM = pl.BlockSpec(memory_space=pltpu.SMEM)

    def place(blocks, whole):
        count = len(blocks)
        held = [] if whole is None else [whole]
        sources = jnp.stack([jnp.stack([off ^ step, z]) for step, z, _ in blocks]).astype(jnp.int32)
        return pl.pallas_call(
            place_kernel(count, rows),
            out_shape=shape(depth, size_x, size_y),
            in_specs=[VMEM] * count + [SMEM] + [HBM] * len(held),
            out_specs=HBM,
            scratch_shapes=[pltpu.SemaphoreType.DMA((count,))],
            input_output_aliases={count + 1: 0} if held else {},
            compiler_params=small,
        )(*(block for *_, block in blocks), sources, *held)

    def swapped(block, bit):
        return lax.ppermute(block, "off", [(i, i ^ bit) for i in range(offs)])

    assert offs & (offs - 1) == 0
    zero = jnp.int32(0)
    bit = offs // 2
    blocks = [(0, zero, part)]
    blocks += [(bit, zero + half * n, swapped(halves[n], bit)) for n in range(2)]
    while bit > 1:
        bit //= 2
        blocks += [(step ^ bit, z, swapped(block, bit)) for step, z, block in blocks]
    return place(blocks[-1:], place(blocks[:-1], None))


def solution(mesh):
    return jax.shard_map(
        shards,
        mesh=mesh,
        in_specs=(P(None, "gx", "gy"), P(None, "gx", "gy")),
        out_specs=P(None, "gx", "gy"),
        check_vma=False,
    )
```

```python
import math

import jax
import jax.numpy as jnp
from jax import lax
from jax.experimental import pallas as pl
from jax.experimental.pallas import tpu as pltpu
from jax.sharding import PartitionSpec as P

EDGE = math.exp(-0.5) / (1.0 + 2.0 * math.exp(-0.5))
GAIN = math.exp(0.5)
SCALE = -(EDGE**3) * math.log2(math.e)
LANES = 128
SUBS = 8
VMEM = pl.BlockSpec(memory_space=pltpu.VMEM)


def partners(count):
    assert count % 2 == 0
    first = [i ^ 1 for i in range(count)]
    second = [(((i + 1) ^ 1) - 1) % count for i in range(count)]
    return first, second


def packed(slices, lane):
    place = (lane + 3) % LANES
    line = jnp.zeros((SUBS, LANES), jnp.float32)
    for z, v in enumerate(slices):
        v = pltpu.roll(v, 16 * z, 1) if z else v
        line = jnp.where((place >= 16 * z) & (place < 16 * z + 6), v, line)
    return line


def lanes():
    return lax.broadcasted_iota(jnp.int32, (SUBS, LANES), 1)


def layer_kernel(volume, layer, arrived):
    off, size_x = lax.axis_index("off"), volume.shape[1]
    at = pl.multiple_of(jnp.where(off == 0, size_x - SUBS, 0), SUBS)
    copy = pltpu.make_async_copy(volume.at[:, pl.ds(at, SUBS), :], layer, arrived)
    copy.start()
    copy.wait()


def window(off, rows, size_x):
    begin = pl.multiple_of(jnp.clip(off * rows - SUBS, 0, size_x - rows - 2 * SUBS), SUBS)

    def block(j):
        at = jnp.clip(off * rows + SUBS * (j - 1), 0, size_x - SUBS) - begin
        return pl.ds(pl.multiple_of(at, SUBS), SUBS)

    return begin, block


def pack_kernel(rows, size_x):
    blocks = rows // SUBS

    def kernel(volume, strength, strips, mine, scale, local, arrived):
        depth = volume.shape[0]
        off = lax.axis_index("off")
        begin, block = window(off, rows, size_x)
        first = pltpu.make_async_copy(
            volume.at[:, pl.ds(begin, rows + 2 * SUBS), :], mine, arrived.at[0]
        )
        start = pl.multiple_of(off * rows, SUBS)
        second = pltpu.make_async_copy(
            strength.at[:, pl.ds(start, rows), :], local, arrived.at[1]
        )
        first.start()
        second.start()
        lane = lanes()
        first.wait()
        for j in range(blocks + 2):
            strips[pl.ds(SUBS * j, SUBS), :] = packed(
                [mine[z, block(j), :] for z in range(depth)], lane
            )
        second.wait()
        for z in range(depth):
            for i in range(blocks):
                scale[z, i] = SCALE / local[z, pl.ds(i, SUBS, stride=blocks), :]

    return kernel


def edges(tall):
    off, offs = lax.axis_index("off"), lax.axis_size("off")
    gx, gxs = lax.axis_index("gx"), lax.axis_size("gx")
    return {0: (off == 0, gx == 0), tall - 1: (off == offs - 1, gx == gxs - 1)}


def join_kernel(strips, layer, joined):
    depth, tall = layer.shape[0], strips.shape[0] // SUBS
    line = packed([layer[z] for z in range(depth)], lanes())
    for j in range(tall):
        at = pl.ds(SUBS * j, SUBS)
        value = strips[at, :]
        for end, (outside, beyond) in edges(tall).items():
            if j == end:
                value = jnp.where(outside, jnp.where(beyond, 0.0, line), value)
        joined[at, :] = value


def three(a, b, c):
    return a + c + GAIN * b


def main_kernel(depth, rows, blocks, size_x):
    wide = blocks + 6
    tall = rows // SUBS + 2

    def kernel(mine, scale, layer, near, far, out, low, high, flat, vals, cent, energy, *sums):
        lane = lanes()
        _, block = window(lax.axis_index("off"), rows, size_x)
        gy, gys = lax.axis_index("gy"), lax.axis_size("gy")
        outer = lane % 16 >= 13
        closed = (outer & (gy == 0)) | ((lane % 16 < 3) & (gy == gys - 1))
        from_near = outer == (gy % 2 == 1)
        ends = edges(tall)

        def side(j):
            at = pl.ds(SUBS * j, SUBS)
            return jnp.where(closed, 0.0, jnp.where(from_near, near[at, :], far[at, :]))

        lines = [side(j) for j in range(tall)]

        def fill(z):
            for r in range(tall):
                at = pl.ds(SUBS * r, SUBS)
                v = mine[z, block(r), :]
                if r in ends:
                    v = jnp.where(ends[r][0], jnp.where(ends[r][1], 0.0, layer[z]), v)
                h = pltpu.roll(lines[r], LANES - 16 * z, 1)
                flat[3, at, :] = v
                for c in range(1, 4):
                    flat[3 + c, at, :] = pltpu.roll(jnp.where(lane < c, h, v), LANES - c, 1)
                    flat[3 - c, at, :] = pltpu.roll(jnp.where(lane >= LANES - c, h, v), c, 1)
            for i in range(wide):
                for c in range(7):
                    v = flat[c, pl.ds(SUBS - 3 + i, SUBS, stride=blocks), :]
                    vals[c, z, i] = v
                    if 2 <= c <= 4 and 2 <= i < wide - 2:
                        cent[c - 2, z, i - 2] = (-2.0 * GAIN if c == 3 else -2.0) * v

        for z in range(depth):
            fill(z)

        def energies(c, _):
            count = blocks + 4
            filtered = []

            def store(z):
                for i in range(count):
                    e = GAIN * filtered[z][i] if 0 <= z < depth else None
                    for y in (z - 1, z + 1):
                        if 0 <= y < depth:
                            e = filtered[y][i] if e is None else e + filtered[y][i]
                    energy[c, z + 1, i] = e

            for z in range(depth):
                line = []
                for i in range(wide):
                    u, v, w = (vals[c + k, z, i] for k in range(3))
                    line.append(three(u * u, v * v, w * w))
                filtered.append([three(*line[i : i + 3]) for i in range(count)])
                store(z - 1)
            store(depth - 1)
            store(depth)
            return 0

        lax.fori_loop(0, 5, energies, 0)

        weigh(depth, blocks, vals, cent, energy, scale, (out, low, high), *sums)

    return kernel


def weigh(depth, blocks, vals, cent, energy, scale, outs, top, total, weighted):
    begin, end = 0, depth
    for z in range(end - begin):
        for i in range(blocks):
            for ref in (top, total, weighted):
                ref[z, i] = jnp.zeros((SUBS, LANES), jnp.float32)

    def offsets(a, b, group):
        first, last = max(0, -a, begin - 1), min(depth, depth - a, end + 1)
        planes = sorted({c + k for c in group for k in range(3)})
        filtered = {}

        def emit(z):
            if not first <= z < last:
                return
            lines = {c: [] for c in group}
            for i in range(blocks + 2):
                v = {k: vals[k, z + a, i + b] for k in planes}
                m = [cent[k, z, i] for k in range(3)]
                for c in group:
                    lines[c].append(m[0] * v[c] + m[2] * v[c + 2] + m[1] * v[c + 1])
            filtered[z] = {
                c: [three(*lines[c][i : i + 3]) for i in range(blocks)] for c in group
            }

        emit(begin - 1)
        emit(begin)
        for z in range(begin, end):
            emit(z + 1)
            for i in range(blocks):
                weights = {}
                for c in group:
                    parts = [filtered[y][c][i] for y in (z - 1, z + 1) if y in filtered]
                    if z in filtered:
                        parts.append(GAIN * filtered[z][c][i])
                    if -1 <= z + a <= depth:
                        parts.append(energy[c, z + a + 1, i + b])
                    if parts:
                        weights[c] = jnp.exp2(scale[z, i] * sum(parts[1:], parts[0]))
                    else:
                        weights[c] = jnp.ones((SUBS, LANES), jnp.float32)
                t = top[z - begin, i]
                s = total[z - begin, i]
                for c in group:
                    t = jnp.maximum(t, weights[c])
                    s = s + weights[c]
                top[z - begin, i] = t
                total[z - begin, i] = s
                if 0 <= z + a < depth:
                    w = weighted[z - begin, i]
                    for c in group:
                        w = w + weights[c] * vals[c + 1, z + a, i + b + 1]
                    weighted[z - begin, i] = w

    for a in range(-2, 3):

        def one(n, _, a=a):
            b = n + jnp.where(n >= 2, 1, 0) if a == 0 else n
            offsets(a, b, range(5))
            return 0

        lax.fori_loop(0, 4 if a == 0 else 5, one, 0)
    offsets(0, 2, (0, 1, 3, 4))

    for z in range(end - begin):
        for i in range(blocks):
            t = top[z, i]
            value = (weighted[z, i] + t * vals[3, z + begin, i + 3]) / (total[z, i] + t)
            part = outs[1] if z < depth // 2 else outs[2]
            for ref, at in ((outs[0], z), (part, z % (depth // 2))):
                ref[at, pl.ds(i, SUBS, stride=blocks), :] = value


def place_kernel(count, rows):
    def kernel(*refs):
        parts, sources, (*_, out, done) = refs[:count], refs[count], refs[count + 1 :]
        copies = []
        for n, part in enumerate(parts):
            at = pl.ds(pl.multiple_of(sources[n, 0] * rows, SUBS), rows)
            for z in range(part.shape[0]):
                target = out.at[sources[n, 1] + z, at, :]
                copies.append(pltpu.make_async_copy(part.at[z], target, done.at[len(copies)]))
                copies[-1].start()
        for copy in copies:
            copy.wait()

    return kernel


def shards(volume, strength):
    depth, size_x, size_y = strength.shape
    gxs, gys, offs = (lax.axis_size(axis) for axis in ("gx", "gy", "off"))
    rows = size_x // offs
    blocks = rows // SUBS
    tall = rows + 2 * SUBS
    assert size_y == LANES and offs > 1
    tile = (SUBS, LANES)
    f32 = jnp.float32
    HBM = pl.BlockSpec(memory_space=pltpu.HBM)

    small = pltpu.CompilerParams(vmem_limit_bytes=4 * 2**20)

    def shape(*sizes):
        return jax.ShapeDtypeStruct(sizes, f32)

    layer = pl.pallas_call(
        layer_kernel,
        out_shape=shape(depth, *tile),
        in_specs=[HBM],
        out_specs=VMEM,
        scratch_shapes=[pltpu.SemaphoreType.DMA],
        compiler_params=small,
    )(volume)
    moves = []
    for x in range(gxs):
        for k in range(offs):
            to = (x + (1 if k == 0 else -1)) % gxs
            moves.append((x * offs + k, to * offs + k))
    layer = lax.ppermute(layer, ("gx", "off"), moves)
    strips, mine, scale = pl.pallas_call(
        pack_kernel(rows, size_x),
        out_shape=[shape(tall, LANES), shape(depth, tall, LANES), shape(depth, blocks, *tile)],
        in_specs=[HBM, HBM],
        out_specs=[VMEM] * 3,
        scratch_shapes=[pltpu.VMEM((depth, rows, LANES), f32), pltpu.SemaphoreType.DMA((2,))],
        cost_estimate=pl.CostEstimate(flops=4_000_000, bytes_accessed=4_000_000, transcendentals=0),
        compiler_params=small,
    )(volume, strength)
    strips = pl.pallas_call(
        join_kernel,
        out_shape=shape(tall, LANES),
        in_specs=[VMEM] * 2,
        out_specs=VMEM,
        compiler_params=small,
    )(strips, layer)
    first, second = partners(gys)
    near = lax.ppermute(strips, "gy", list(enumerate(first)))
    far = lax.ppermute(strips, "gy", list(enumerate(second)))
    half = depth // 2
    part, *halves = pl.pallas_call(
        main_kernel(depth, rows, blocks, size_x),
        out_shape=[shape(depth, rows, size_y)] + [shape(half, rows, size_y)] * 2,
        in_specs=[VMEM] * 5,
        out_specs=[VMEM] * 3,
        scratch_shapes=[
            pltpu.VMEM((7, tall, LANES), f32),
            pltpu.VMEM((7, depth, blocks + 6) + tile, f32),
            pltpu.VMEM((3, depth, blocks + 2) + tile, f32),
            pltpu.VMEM((5, depth + 2, blocks + 4) + tile, f32),
        ]
        + [pltpu.VMEM((depth, blocks) + tile, f32)] * 3,
        compiler_params=pltpu.CompilerParams(vmem_limit_bytes=16 * 2**20),
    )(mine, scale, layer, near, far)

    off = lax.axis_index("off")
    SMEM = pl.BlockSpec(memory_space=pltpu.SMEM)

    def place(blocks, whole):
        count = len(blocks)
        held = [] if whole is None else [whole]
        sources = jnp.stack([jnp.stack([off ^ step, z]) for step, z, _ in blocks]).astype(jnp.int32)
        return pl.pallas_call(
            place_kernel(count, rows),
            out_shape=shape(depth, size_x, size_y),
            in_specs=[VMEM] * count + [SMEM] + [HBM] * len(held),
            out_specs=HBM,
            scratch_shapes=[pltpu.SemaphoreType.DMA((sum(len(b) for *_, b in blocks),))],
            input_output_aliases={count + 1: 0} if held else {},
            compiler_params=small,
        )(*(block for *_, block in blocks), sources, *held)

    def swapped(block, bit):
        return lax.ppermute(block, "off", [(i, i ^ bit) for i in range(offs)])

    assert offs & (offs - 1) == 0
    zero = jnp.int32(0)
    bit = offs // 2
    blocks = [(0, zero, part)]
    blocks += [(bit, zero + half * n, swapped(halves[n], bit)) for n in range(2)]
    while bit > 1:
        bit //= 2
        blocks += [(step ^ bit, z, swapped(block, bit)) for step, z, block in blocks]
    return place(blocks[-2:], place(blocks[:-2], None))


def solution(mesh):
    return jax.shard_map(
        shards,
        mesh=mesh,
        in_specs=(P(None, "gx", "gy"), P(None, "gx", "gy")),
        out_specs=P(None, "gx", "gy"),
        check_vma=False,
    )
```

```python
import math

import jax
import jax.numpy as jnp
from jax import lax
from jax.experimental import pallas as pl
from jax.experimental.pallas import tpu as pltpu
from jax.sharding import PartitionSpec as P

EDGE = math.exp(-0.5) / (1.0 + 2.0 * math.exp(-0.5))
GAIN = math.exp(0.5)
SCALE = -(EDGE**3) * math.log2(math.e)
LANES = 128
SUBS = 8
VMEM = pl.BlockSpec(memory_space=pltpu.VMEM)


def partners(count):
    assert count % 2 == 0
    first = [i ^ 1 for i in range(count)]
    second = [(((i + 1) ^ 1) - 1) % count for i in range(count)]
    return first, second


def packed(slices, lane):
    place = (lane + 3) % LANES
    line = jnp.zeros((SUBS, LANES), jnp.float32)
    for z, v in enumerate(slices):
        v = pltpu.roll(v, 16 * z, 1) if z else v
        line = jnp.where((place >= 16 * z) & (place < 16 * z + 6), v, line)
    return line


def lanes():
    return lax.broadcasted_iota(jnp.int32, (SUBS, LANES), 1)


def layer_kernel(volume, layer, arrived):
    off, size_x = lax.axis_index("off"), volume.shape[1]
    at = pl.multiple_of(jnp.where(off == 0, size_x - SUBS, 0), SUBS)
    copy = pltpu.make_async_copy(volume.at[:, pl.ds(at, SUBS), :], layer, arrived)
    copy.start()
    copy.wait()


def window(off, rows, size_x):
    begin = pl.multiple_of(jnp.clip(off * rows - SUBS, 0, size_x - rows - 2 * SUBS), SUBS)

    def block(j):
        at = jnp.clip(off * rows + SUBS * (j - 1), 0, size_x - SUBS) - begin
        return pl.ds(pl.multiple_of(at, SUBS), SUBS)

    return begin, block


def pack_kernel(rows, size_x):
    blocks = rows // SUBS

    def kernel(volume, strength, strips, mine, scale, local, arrived):
        depth = volume.shape[0]
        off = lax.axis_index("off")
        begin, block = window(off, rows, size_x)
        first = pltpu.make_async_copy(
            volume.at[:, pl.ds(begin, rows + 2 * SUBS), :], mine, arrived.at[0]
        )
        start = pl.multiple_of(off * rows, SUBS)
        second = pltpu.make_async_copy(
            strength.at[:, pl.ds(start, rows), :], local, arrived.at[1]
        )
        first.start()
        second.start()
        lane = lanes()
        first.wait()
        for j in range(blocks + 2):
            strips[pl.ds(SUBS * j, SUBS), :] = packed(
                [mine[z, block(j), :] for z in range(depth)], lane
            )
        second.wait()
        for z in range(depth):
            for i in range(blocks):
                scale[z, i] = SCALE / local[z, pl.ds(i, SUBS, stride=blocks), :]

    return kernel


def edges(tall):
    off, offs = lax.axis_index("off"), lax.axis_size("off")
    gx, gxs = lax.axis_index("gx"), lax.axis_size("gx")
    return {0: (off == 0, gx == 0), tall - 1: (off == offs - 1, gx == gxs - 1)}


def join_kernel(strips, layer, joined):
    depth, tall = layer.shape[0], strips.shape[0] // SUBS
    line = packed([layer[z] for z in range(depth)], lanes())
    for j in range(tall):
        at = pl.ds(SUBS * j, SUBS)
        value = strips[at, :]
        for end, (outside, beyond) in edges(tall).items():
            if j == end:
                value = jnp.where(outside, jnp.where(beyond, 0.0, line), value)
        joined[at, :] = value


def three(a, b, c):
    return a + c + GAIN * b


def main_kernel(depth, rows, blocks, size_x):
    wide = blocks + 6
    tall = rows // SUBS + 2

    def kernel(mine, scale, layer, near, far, out, low, high, flat, vals, cent, energy, *sums):
        lane = lanes()
        _, block = window(lax.axis_index("off"), rows, size_x)
        gy, gys = lax.axis_index("gy"), lax.axis_size("gy")
        outer = lane % 16 >= 13
        closed = (outer & (gy == 0)) | ((lane % 16 < 3) & (gy == gys - 1))
        from_near = outer == (gy % 2 == 1)
        ends = edges(tall)

        def side(j):
            at = pl.ds(SUBS * j, SUBS)
            return jnp.where(closed, 0.0, jnp.where(from_near, near[at, :], far[at, :]))

        lines = [side(j) for j in range(tall)]

        def fill(z):
            for r in range(tall):
                at = pl.ds(SUBS * r, SUBS)
                v = mine[z, block(r), :]
                if r in ends:
                    v = jnp.where(ends[r][0], jnp.where(ends[r][1], 0.0, layer[z]), v)
                h = pltpu.roll(lines[r], LANES - 16 * z, 1)
                flat[z, 3, at, :] = v
                for c in range(1, 4):
                    flat[z, 3 + c, at, :] = pltpu.roll(jnp.where(lane < c, h, v), LANES - c, 1)
                    flat[z, 3 - c, at, :] = pltpu.roll(jnp.where(lane >= LANES - c, h, v), c, 1)
            for i in range(wide):
                for c in range(7):
                    v = flat[z, c, pl.ds(SUBS - 3 + i, SUBS, stride=blocks), :]
                    vals[c, z, i] = v
                    if 2 <= c <= 4 and 2 <= i < wide - 2:
                        cent[c - 2, z, i - 2] = (-2.0 * GAIN if c == 3 else -2.0) * v

        for z in range(depth):
            fill(z)

        def energies(c, _):
            count = blocks + 4
            filtered = []

            def store(z):
                for i in range(count):
                    e = GAIN * filtered[z][i] if 0 <= z < depth else None
                    for y in (z - 1, z + 1):
                        if 0 <= y < depth:
                            e = filtered[y][i] if e is None else e + filtered[y][i]
                    energy[c, z + 1, i] = e

            for z in range(depth):
                line = []
                for i in range(wide):
                    u, v, w = (vals[c + k, z, i] for k in range(3))
                    line.append(three(u * u, v * v, w * w))
                filtered.append([three(*line[i : i + 3]) for i in range(count)])
                store(z - 1)
            store(depth - 1)
            store(depth)
            return 0

        lax.fori_loop(0, 5, energies, 0)

        weigh(depth, blocks, vals, cent, energy, scale, (out, low, high), *sums)

    return kernel


def weigh(depth, blocks, vals, cent, energy, scale, outs, top, total, weighted):
    begin, end = 0, depth
    for z in range(end - begin):
        for i in range(blocks):
            for ref in (top, total, weighted):
                ref[z, i] = jnp.zeros((SUBS, LANES), jnp.float32)

    def offsets(a, b, group):
        first, last = max(0, -a, begin - 1), min(depth, depth - a, end + 1)
        planes = sorted({c + k for c in group for k in range(3)})
        filtered = {}

        def emit(z):
            if not first <= z < last:
                return
            lines = {c: [] for c in group}
            for i in range(blocks + 2):
                v = {k: vals[k, z + a, i + b] for k in planes}
                m = [cent[k, z, i] for k in range(3)]
                for c in group:
                    lines[c].append(m[0] * v[c] + m[2] * v[c + 2] + m[1] * v[c + 1])
            filtered[z] = {
                c: [three(*lines[c][i : i + 3]) for i in range(blocks)] for c in group
            }

        emit(begin - 1)
        emit(begin)
        for z in range(begin, end):
            emit(z + 1)
            for i in range(blocks):
                weights = {}
                for c in group:
                    parts = [filtered[y][c][i] for y in (z - 1, z + 1) if y in filtered]
                    if z in filtered:
                        parts.append(GAIN * filtered[z][c][i])
                    if -1 <= z + a <= depth:
                        parts.append(energy[c, z + a + 1, i + b])
                    if parts:
                        weights[c] = jnp.exp2(scale[z, i] * sum(parts[1:], parts[0]))
                    else:
                        weights[c] = jnp.ones((SUBS, LANES), jnp.float32)
                t = top[z - begin, i]
                s = total[z - begin, i]
                for c in group:
                    t = jnp.maximum(t, weights[c])
                    s = s + weights[c]
                top[z - begin, i] = t
                total[z - begin, i] = s
                if 0 <= z + a < depth:
                    w = weighted[z - begin, i]
                    for c in group:
                        w = w + weights[c] * vals[c + 1, z + a, i + b + 1]
                    weighted[z - begin, i] = w

    for a in range(-2, 3):

        def one(n, _, a=a):
            b = n + jnp.where(n >= 2, 1, 0) if a == 0 else n
            offsets(a, b, range(5))
            return 0

        lax.fori_loop(0, 4 if a == 0 else 5, one, 0)
    offsets(0, 2, (0, 1, 3, 4))

    for z in range(end - begin):
        for i in range(blocks):
            t = top[z, i]
            value = (weighted[z, i] + t * vals[3, z + begin, i + 3]) / (total[z, i] + t)
            part = outs[1] if z < depth // 2 else outs[2]
            for ref, at in ((outs[0], z), (part, z % (depth // 2))):
                ref[at, pl.ds(i, SUBS, stride=blocks), :] = value


def place_kernel(sources, rows):
    def kernel(*refs):
        parts, (*_, out, done) = refs[: len(sources)], refs[len(sources) :]
        off = lax.axis_index("off")
        copies = []
        for n, (part, (step, z)) in enumerate(zip(parts, sources)):
            at = pl.ds(pl.multiple_of((off ^ step) * rows, SUBS), rows)
            target = out.at[z : z + part.shape[0], at, :]
            copies.append(pltpu.make_async_copy(part, target, done.at[n]))
            copies[n].start()
        for copy in copies:
            copy.wait()

    return kernel


def shards(volume, strength):
    depth, size_x, size_y = strength.shape
    gxs, gys, offs = (lax.axis_size(axis) for axis in ("gx", "gy", "off"))
    rows = size_x // offs
    blocks = rows // SUBS
    tall = rows + 2 * SUBS
    assert size_y == LANES and offs > 1
    tile = (SUBS, LANES)
    f32 = jnp.float32
    HBM = pl.BlockSpec(memory_space=pltpu.HBM)

    small = pltpu.CompilerParams(vmem_limit_bytes=4 * 2**20)

    def shape(*sizes):
        return jax.ShapeDtypeStruct(sizes, f32)

    layer = pl.pallas_call(
        layer_kernel,
        out_shape=shape(depth, *tile),
        in_specs=[HBM],
        out_specs=VMEM,
        scratch_shapes=[pltpu.SemaphoreType.DMA],
        compiler_params=small,
    )(volume)
    moves = []
    for x in range(gxs):
        for k in range(offs):
            to = (x + (1 if k == 0 else -1)) % gxs
            moves.append((x * offs + k, to * offs + k))
    layer = lax.ppermute(layer, ("gx", "off"), moves)
    strips, mine, scale = pl.pallas_call(
        pack_kernel(rows, size_x),
        out_shape=[shape(tall, LANES), shape(depth, tall, LANES), shape(depth, blocks, *tile)],
        in_specs=[HBM, HBM],
        out_specs=[VMEM] * 3,
        scratch_shapes=[pltpu.VMEM((depth, rows, LANES), f32), pltpu.SemaphoreType.DMA((2,))],
        cost_estimate=pl.CostEstimate(flops=4_000_000, bytes_accessed=4_000_000, transcendentals=0),
        compiler_params=small,
    )(volume, strength)
    strips = pl.pallas_call(
        join_kernel,
        out_shape=shape(tall, LANES),
        in_specs=[VMEM] * 2,
        out_specs=VMEM,
        compiler_params=small,
    )(strips, layer)
    first, second = partners(gys)
    near = lax.ppermute(strips, "gy", list(enumerate(first)))
    far = lax.ppermute(strips, "gy", list(enumerate(second)))
    half = depth // 2
    part, *halves = pl.pallas_call(
        main_kernel(depth, rows, blocks, size_x),
        out_shape=[shape(depth, rows, size_y)] + [shape(half, rows, size_y)] * 2,
        in_specs=[VMEM] * 5,
        out_specs=[VMEM] * 3,
        scratch_shapes=[
            pltpu.VMEM((depth, 7, tall, LANES), f32),
            pltpu.VMEM((7, depth, blocks + 6) + tile, f32),
            pltpu.VMEM((3, depth, blocks + 2) + tile, f32),
            pltpu.VMEM((5, depth + 2, blocks + 4) + tile, f32),
        ]
        + [pltpu.VMEM((depth, blocks) + tile, f32)] * 3,
        compiler_params=pltpu.CompilerParams(vmem_limit_bytes=16 * 2**20),
    )(mine, scale, layer, near, far)

    def place(blocks, whole):
        count = len(blocks)
        held = [] if whole is None else [whole]
        return pl.pallas_call(
            place_kernel([source for source, _ in blocks], rows),
            out_shape=shape(depth, size_x, size_y),
            in_specs=[VMEM] * count + [HBM] * len(held),
            out_specs=HBM,
            scratch_shapes=[pltpu.SemaphoreType.DMA((count,))],
            input_output_aliases={count: 0} if held else {},
            compiler_params=small,
        )(*(block for _, block in blocks), *held)

    def swapped(block, bit):
        return lax.ppermute(block, "off", [(i, i ^ bit) for i in range(offs)])

    assert offs & (offs - 1) == 0
    bit = offs // 2
    blocks = [((0, 0), part)]
    blocks += [((bit, half * n), swapped(halves[n], bit)) for n in range(2)]
    while bit > 1:
        bit //= 2
        blocks += [((step ^ bit, z), swapped(block, bit)) for (step, z), block in blocks]
    return place(blocks[-2:], place(blocks[:-2], None))


def solution(mesh):
    return jax.shard_map(
        shards,
        mesh=mesh,
        in_specs=(P(None, "gx", "gy"), P(None, "gx", "gy")),
        out_specs=P(None, "gx", "gy"),
        check_vma=False,
    )
```

```python
import math

import jax
import jax.numpy as jnp
from jax import lax
from jax.experimental import pallas as pl
from jax.experimental.pallas import tpu as pltpu
from jax.sharding import PartitionSpec as P

EDGE = math.exp(-0.5) / (1.0 + 2.0 * math.exp(-0.5))
GAIN = math.exp(0.5)
SCALE = -(EDGE**3) * math.log2(math.e)
LANES = 128
SUBS = 8
VMEM = pl.BlockSpec(memory_space=pltpu.VMEM)


def partners(count):
    assert count % 2 == 0
    first = [i ^ 1 for i in range(count)]
    second = [(((i + 1) ^ 1) - 1) % count for i in range(count)]
    return first, second


def packed(slices, lane):
    place = (lane + 3) % LANES
    line = jnp.zeros((SUBS, LANES), jnp.float32)
    for z, v in enumerate(slices):
        v = pltpu.roll(v, 16 * z, 1) if z else v
        line = jnp.where((place >= 16 * z) & (place < 16 * z + 6), v, line)
    return line


def lanes():
    return lax.broadcasted_iota(jnp.int32, (SUBS, LANES), 1)


def layer_kernel(volume, layer, arrived):
    off, size_x = lax.axis_index("off"), volume.shape[1]
    at = pl.multiple_of(jnp.where(off == 0, size_x - SUBS, 0), SUBS)
    copy = pltpu.make_async_copy(volume.at[:, pl.ds(at, SUBS), :], layer, arrived)
    copy.start()
    copy.wait()


def window(off, rows, size_x):
    begin = pl.multiple_of(jnp.clip(off * rows - SUBS, 0, size_x - rows - 2 * SUBS), SUBS)

    def block(j):
        at = jnp.clip(off * rows + SUBS * (j - 1), 0, size_x - SUBS) - begin
        return pl.ds(pl.multiple_of(at, SUBS), SUBS)

    return begin, block


def pack_kernel(rows, size_x):
    blocks = rows // SUBS

    def kernel(volume, strength, strips, mine, scale, local, arrived):
        depth = volume.shape[0]
        off = lax.axis_index("off")
        begin, block = window(off, rows, size_x)
        first = pltpu.make_async_copy(
            volume.at[:, pl.ds(begin, rows + 2 * SUBS), :], mine, arrived.at[0]
        )
        start = pl.multiple_of(off * rows, SUBS)
        second = pltpu.make_async_copy(
            strength.at[:, pl.ds(start, rows), :], local, arrived.at[1]
        )
        first.start()
        second.start()
        lane = lanes()
        first.wait()
        for j in range(blocks + 2):
            strips[pl.ds(SUBS * j, SUBS), :] = packed(
                [mine[z, block(j), :] for z in range(depth)], lane
            )
        second.wait()
        for z in range(depth):
            for i in range(blocks):
                scale[z, i] = SCALE / local[z, pl.ds(i, SUBS, stride=blocks), :]

    return kernel


def edges(tall):
    off, offs = lax.axis_index("off"), lax.axis_size("off")
    gx, gxs = lax.axis_index("gx"), lax.axis_size("gx")
    return {0: (off == 0, gx == 0), tall - 1: (off == offs - 1, gx == gxs - 1)}


def join_kernel(strips, layer, joined):
    depth, tall = layer.shape[0], strips.shape[0] // SUBS
    line = packed([layer[z] for z in range(depth)], lanes())
    for j in range(tall):
        at = pl.ds(SUBS * j, SUBS)
        value = strips[at, :]
        for end, (outside, beyond) in edges(tall).items():
            if j == end:
                value = jnp.where(outside, jnp.where(beyond, 0.0, line), value)
        joined[at, :] = value


def three(a, b, c):
    return a + c + GAIN * b


def shift_kernel(rows, size_x):
    def kernel(mine, layer, moved):
        depth, tall = mine.shape[0], mine.shape[1] // SUBS
        _, block = window(lax.axis_index("off"), rows, size_x)
        ends = edges(tall)
        for z in range(depth):
            for r in range(tall):
                v = mine[z, block(r), :]
                if r in ends:
                    v = jnp.where(ends[r][0], jnp.where(ends[r][1], 0.0, layer[z]), v)
                for c in range(7):
                    shift = (3 - c) % LANES
                    moved[z, c, pl.ds(SUBS * r, SUBS), :] = pltpu.roll(v, shift, 1) if shift else v

    return kernel


def main_kernel(depth, rows, blocks):
    wide = blocks + 6
    tall = rows // SUBS + 2

    def kernel(moved, scale, near, far, low, high, flat, vals, cent, energy, *sums):
        lane = lanes()
        gy, gys = lax.axis_index("gy"), lax.axis_size("gy")
        outer = lane % 16 >= 13
        closed = (outer & (gy == 0)) | ((lane % 16 < 3) & (gy == gys - 1))
        from_near = outer == (gy % 2 == 1)

        def side(j):
            at = pl.ds(SUBS * j, SUBS)
            line = jnp.where(closed, 0.0, jnp.where(from_near, near[at, :], far[at, :]))
            return [
                jnp.where(outer, pltpu.roll(line, LANES - c, 1), pltpu.roll(line, c, 1))
                for c in range(1, 4)
            ]

        lines = [side(j) for j in range(tall)]

        def fill(z):
            for r in range(tall):
                at = pl.ds(SUBS * r, SUBS)
                flat[z, 3, at, :] = moved[z, 3, at, :]
                for c in range(1, 4):
                    h = pltpu.roll(lines[r][c - 1], LANES - 16 * z, 1) if z else lines[r][c - 1]
                    flat[z, 3 + c, at, :] = jnp.where(lane >= LANES - c, h, moved[z, 3 + c, at, :])
                    flat[z, 3 - c, at, :] = jnp.where(lane < c, h, moved[z, 3 - c, at, :])
            for i in range(wide):
                for c in range(7):
                    v = flat[z, c, pl.ds(SUBS - 3 + i, SUBS, stride=blocks), :]
                    vals[c, z, i] = v
                    if 2 <= c <= 4 and 2 <= i < wide - 2:
                        cent[c - 2, z, i - 2] = (-2.0 * GAIN if c == 3 else -2.0) * v

        for z in range(depth):
            fill(z)

        def energies(c):
            count = blocks + 4
            filtered = []

            def store(z):
                for i in range(count):
                    e = GAIN * filtered[z][i] if 0 <= z < depth else None
                    for y in (z - 1, z + 1):
                        if 0 <= y < depth:
                            e = filtered[y][i] if e is None else e + filtered[y][i]
                    energy[c, z + 1, i] = e

            for z in range(depth):
                line = []
                for i in range(wide):
                    u, v, w = (vals[c + k, z, i] for k in range(3))
                    line.append(three(u * u, v * v, w * w))
                filtered.append([three(*line[i : i + 3]) for i in range(count)])
                store(z - 1)
            store(depth - 1)
            store(depth)

        for c in range(5):
            energies(c)

        weigh(depth, blocks, vals, cent, energy, scale, (low, high), *sums)

    return kernel


def weigh(depth, blocks, vals, cent, energy, scale, outs, top, total, weighted):
    begin, end = 0, depth
    for z in range(end - begin):
        for i in range(blocks):
            for ref in (top, total, weighted):
                ref[z, i] = jnp.zeros((SUBS, LANES), jnp.float32)

    def offsets(a, b, group):
        first, last = max(0, -a, begin - 1), min(depth, depth - a, end + 1)
        planes = sorted({c + k for c in group for k in range(3)})
        filtered = {}

        def emit(z):
            if not first <= z < last:
                return
            lines = {c: [] for c in group}
            for i in range(blocks + 2):
                v = {k: vals[k, z + a, i + b] for k in planes}
                m = [cent[k, z, i] for k in range(3)]
                for c in group:
                    lines[c].append(m[0] * v[c] + m[2] * v[c + 2] + m[1] * v[c + 1])
            filtered[z] = {
                c: [three(*lines[c][i : i + 3]) for i in range(blocks)] for c in group
            }

        emit(begin - 1)
        emit(begin)
        for z in range(begin, end):
            emit(z + 1)
            for i in range(blocks):
                weights = {}
                for c in group:
                    parts = [filtered[y][c][i] for y in (z - 1, z + 1) if y in filtered]
                    if z in filtered:
                        parts.append(GAIN * filtered[z][c][i])
                    if -1 <= z + a <= depth:
                        parts.append(energy[c, z + a + 1, i + b])
                    if parts:
                        weights[c] = jnp.exp2(scale[z, i] * sum(parts[1:], parts[0]))
                    else:
                        weights[c] = jnp.ones((SUBS, LANES), jnp.float32)
                t = top[z - begin, i]
                s = total[z - begin, i]
                for c in group:
                    t = jnp.maximum(t, weights[c])
                    s = s + weights[c]
                top[z - begin, i] = t
                total[z - begin, i] = s
                if 0 <= z + a < depth:
                    w = weighted[z - begin, i]
                    for c in group:
                        w = w + weights[c] * vals[c + 1, z + a, i + b + 1]
                    weighted[z - begin, i] = w

    for a in range(-2, 3):

        def one(n, _, a=a):
            b = n + jnp.where(n >= 2, 1, 0) if a == 0 else n
            offsets(a, b, range(5))
            return 0

        lax.fori_loop(0, 4 if a == 0 else 5, one, 0)
    offsets(0, 2, (0, 1, 3, 4))

    for z in range(end - begin):
        for i in range(blocks):
            t = top[z, i]
            value = (weighted[z, i] + t * vals[3, z + begin, i + 3]) / (total[z, i] + t)
            part = outs[z // (depth // 2)]
            part[z % (depth // 2), pl.ds(i, SUBS, stride=blocks), :] = value


def place_kernel(sources, rows):
    def kernel(*refs):
        parts, (*_, out, done) = refs[: len(sources)], refs[len(sources) :]
        off = lax.axis_index("off")
        copies = []
        for n, (part, (step, z)) in enumerate(zip(parts, sources)):
            at = pl.ds(pl.multiple_of((off ^ step) * rows, SUBS), rows)
            target = out.at[z : z + part.shape[0], at, :]
            copies.append(pltpu.make_async_copy(part, target, done.at[n]))
            copies[n].start()
        for copy in copies:
            copy.wait()

    return kernel


def shards(volume, strength):
    depth, size_x, size_y = strength.shape
    gxs, gys, offs = (lax.axis_size(axis) for axis in ("gx", "gy", "off"))
    rows = size_x // offs
    blocks = rows // SUBS
    tall = rows + 2 * SUBS
    assert size_y == LANES and offs > 1
    tile = (SUBS, LANES)
    f32 = jnp.float32
    HBM = pl.BlockSpec(memory_space=pltpu.HBM)

    small = pltpu.CompilerParams(vmem_limit_bytes=4 * 2**20)

    def shape(*sizes):
        return jax.ShapeDtypeStruct(sizes, f32)

    layer = pl.pallas_call(
        layer_kernel,
        out_shape=shape(depth, *tile),
        in_specs=[HBM],
        out_specs=VMEM,
        scratch_shapes=[pltpu.SemaphoreType.DMA],
        compiler_params=small,
    )(volume)
    moves = []
    for x in range(gxs):
        for k in range(offs):
            to = (x + (1 if k == 0 else -1)) % gxs
            moves.append((x * offs + k, to * offs + k))
    layer = lax.ppermute(layer, ("gx", "off"), moves)
    strips, mine, scale = pl.pallas_call(
        pack_kernel(rows, size_x),
        out_shape=[shape(tall, LANES), shape(depth, tall, LANES), shape(depth, blocks, *tile)],
        in_specs=[HBM, HBM],
        out_specs=[VMEM] * 3,
        scratch_shapes=[pltpu.VMEM((depth, rows, LANES), f32), pltpu.SemaphoreType.DMA((2,))],
        cost_estimate=pl.CostEstimate(flops=4_000_000, bytes_accessed=4_000_000, transcendentals=0),
        compiler_params=small,
    )(volume, strength)
    strips = pl.pallas_call(
        join_kernel,
        out_shape=shape(tall, LANES),
        in_specs=[VMEM] * 2,
        out_specs=VMEM,
        compiler_params=small,
    )(strips, layer)
    first, second = partners(gys)
    near = lax.ppermute(strips, "gy", list(enumerate(first)))
    far = lax.ppermute(strips, "gy", list(enumerate(second)))
    moved = pl.pallas_call(
        shift_kernel(rows, size_x),
        out_shape=shape(depth, 7, tall, LANES),
        in_specs=[VMEM] * 2,
        out_specs=VMEM,
        cost_estimate=pl.CostEstimate(flops=4_000_000, bytes_accessed=4_000_000, transcendentals=0),
        compiler_params=small,
    )(mine, layer)
    half = depth // 2
    halves = pl.pallas_call(
        main_kernel(depth, rows, blocks),
        out_shape=[shape(half, rows, size_y)] * 2,
        in_specs=[VMEM] * 4,
        out_specs=[VMEM] * 2,
        scratch_shapes=[
            pltpu.VMEM((depth, 7, tall, LANES), f32),
            pltpu.VMEM((7, depth, blocks + 6) + tile, f32),
            pltpu.VMEM((3, depth, blocks + 2) + tile, f32),
            pltpu.VMEM((5, depth + 2, blocks + 4) + tile, f32),
        ]
        + [pltpu.VMEM((depth, blocks) + tile, f32)] * 3,
        compiler_params=pltpu.CompilerParams(vmem_limit_bytes=16 * 2**20),
    )(moved, scale, near, far)

    def place(blocks, whole):
        count = len(blocks)
        held = [] if whole is None else [whole]
        return pl.pallas_call(
            place_kernel([source for source, _ in blocks], rows),
            out_shape=shape(depth, size_x, size_y),
            in_specs=[VMEM] * count + [HBM] * len(held),
            out_specs=HBM,
            scratch_shapes=[pltpu.SemaphoreType.DMA((count,))],
            input_output_aliases={count: 0} if held else {},
            compiler_params=small,
        )(*(block for _, block in blocks), *held)

    def swapped(block, bit):
        return lax.ppermute(block, "off", [(i, i ^ bit) for i in range(offs)])

    assert offs & (offs - 1) == 0
    bit = offs // 2
    blocks = [((0, half * n), halves[n]) for n in range(2)]
    blocks += [((bit, half * n), swapped(halves[n], bit)) for n in range(2)]
    while bit > 1:
        bit //= 2
        blocks += [((step ^ bit, z), swapped(block, bit)) for (step, z), block in blocks]
    return place(blocks[-2:], place(blocks[:-2], None))


def solution(mesh):
    return jax.shard_map(
        shards,
        mesh=mesh,
        in_specs=(P(None, "gx", "gy"), P(None, "gx", "gy")),
        out_specs=P(None, "gx", "gy"),
        check_vma=False,
    )
```

```python
import math

import jax
import jax.numpy as jnp
from jax import lax
from jax.experimental import pallas as pl
from jax.experimental.pallas import tpu as pltpu
from jax.sharding import PartitionSpec as P

EDGE = math.exp(-0.5) / (1.0 + 2.0 * math.exp(-0.5))
GAIN = math.exp(0.5)
SCALE = -(EDGE**3) * math.log2(math.e)
LANES = 128
SUBS = 8
VMEM = pl.BlockSpec(memory_space=pltpu.VMEM)


def partners(count):
    assert count % 2 == 0
    first = [i ^ 1 for i in range(count)]
    second = [(((i + 1) ^ 1) - 1) % count for i in range(count)]
    return first, second


def packed(slices, lane):
    place = (lane + 3) % LANES
    line = jnp.zeros((SUBS, LANES), jnp.float32)
    for z, v in enumerate(slices):
        v = pltpu.roll(v, 16 * z, 1) if z else v
        line = jnp.where((place >= 16 * z) & (place < 16 * z + 6), v, line)
    return line


def lanes():
    return lax.broadcasted_iota(jnp.int32, (SUBS, LANES), 1)


def layer_kernel(volume, layer, arrived):
    off, size_x = lax.axis_index("off"), volume.shape[1]
    at = pl.multiple_of(jnp.where(off == 0, size_x - SUBS, 0), SUBS)
    copy = pltpu.make_async_copy(volume.at[:, pl.ds(at, SUBS), :], layer, arrived)
    copy.start()
    copy.wait()


def window(off, rows, size_x):
    begin = pl.multiple_of(jnp.clip(off * rows - SUBS, 0, size_x - rows - 2 * SUBS), SUBS)

    def block(j):
        at = jnp.clip(off * rows + SUBS * (j - 1), 0, size_x - SUBS) - begin
        return pl.ds(pl.multiple_of(at, SUBS), SUBS)

    return begin, block


def pack_kernel(rows, size_x):
    blocks = rows // SUBS

    def kernel(volume, strength, strips, mine, scale, local, arrived):
        depth = volume.shape[0]
        off = lax.axis_index("off")
        begin, block = window(off, rows, size_x)
        first = pltpu.make_async_copy(
            volume.at[:, pl.ds(begin, rows + 2 * SUBS), :], mine, arrived.at[0]
        )
        start = pl.multiple_of(off * rows, SUBS)
        second = pltpu.make_async_copy(
            strength.at[:, pl.ds(start, rows), :], local, arrived.at[1]
        )
        first.start()
        second.start()
        lane = lanes()
        first.wait()
        for j in range(blocks + 2):
            strips[pl.ds(SUBS * j, SUBS), :] = packed(
                [mine[z, block(j), :] for z in range(depth)], lane
            )
        second.wait()
        for z in range(depth):
            for i in range(blocks):
                scale[z, i] = SCALE / local[z, pl.ds(i, SUBS, stride=blocks), :]

    return kernel


def edges(tall):
    off, offs = lax.axis_index("off"), lax.axis_size("off")
    gx, gxs = lax.axis_index("gx"), lax.axis_size("gx")
    return {0: (off == 0, gx == 0), tall - 1: (off == offs - 1, gx == gxs - 1)}


def join_kernel(strips, layer, joined):
    depth, tall = layer.shape[0], strips.shape[0] // SUBS
    line = packed([layer[z] for z in range(depth)], lanes())
    for j in range(tall):
        at = pl.ds(SUBS * j, SUBS)
        value = strips[at, :]
        for end, (outside, beyond) in edges(tall).items():
            if j == end:
                value = jnp.where(outside, jnp.where(beyond, 0.0, line), value)
        joined[at, :] = value


def three(a, b, c):
    return a + c + GAIN * b


def shift_kernel(rows, size_x):
    def kernel(mine, layer, moved):
        depth, tall = mine.shape[0], mine.shape[1] // SUBS
        _, block = window(lax.axis_index("off"), rows, size_x)
        ends = edges(tall)
        for z in range(depth):
            for r in range(tall):
                v = mine[z, block(r), :]
                if r in ends:
                    v = jnp.where(ends[r][0], jnp.where(ends[r][1], 0.0, layer[z]), v)
                for c in range(7):
                    shift = (3 - c) % LANES
                    moved[z, c, pl.ds(SUBS * r, SUBS), :] = pltpu.roll(v, shift, 1) if shift else v

    return kernel


def main_kernel(depth, rows, blocks):
    wide = blocks + 6
    tall = rows // SUBS + 2

    def kernel(moved, scale, near, far, out, low, high, flat, vals, cent, energy, *sums):
        lane = lanes()
        gy, gys = lax.axis_index("gy"), lax.axis_size("gy")
        outer = lane % 16 >= 13
        closed = (outer & (gy == 0)) | ((lane % 16 < 3) & (gy == gys - 1))
        from_near = outer == (gy % 2 == 1)

        def side(j):
            at = pl.ds(SUBS * j, SUBS)
            line = jnp.where(closed, 0.0, jnp.where(from_near, near[at, :], far[at, :]))
            return [
                jnp.where(outer, pltpu.roll(line, LANES - c, 1), pltpu.roll(line, c, 1))
                for c in range(1, 4)
            ]

        lines = [side(j) for j in range(tall)]

        def fill(z):
            for r in range(tall):
                at = pl.ds(SUBS * r, SUBS)
                flat[z, 3, at, :] = moved[z, 3, at, :]
                for c in range(1, 4):
                    h = pltpu.roll(lines[r][c - 1], LANES - 16 * z, 1) if z else lines[r][c - 1]
                    flat[z, 3 + c, at, :] = jnp.where(lane >= LANES - c, h, moved[z, 3 + c, at, :])
                    flat[z, 3 - c, at, :] = jnp.where(lane < c, h, moved[z, 3 - c, at, :])
            for i in range(wide):
                for c in range(7):
                    v = flat[z, c, pl.ds(SUBS - 3 + i, SUBS, stride=blocks), :]
                    vals[c, z, i] = v
                    if 2 <= c <= 4 and 2 <= i < wide - 2:
                        cent[c - 2, z, i - 2] = (-2.0 * GAIN if c == 3 else -2.0) * v

        for z in range(depth):
            fill(z)

        def energies(c):
            count = blocks + 4
            filtered = []

            def store(z):
                for i in range(count):
                    e = GAIN * filtered[z][i] if 0 <= z < depth else None
                    for y in (z - 1, z + 1):
                        if 0 <= y < depth:
                            e = filtered[y][i] if e is None else e + filtered[y][i]
                    energy[c, z + 1, i] = e

            for z in range(depth):
                line = []
                for i in range(wide):
                    u, v, w = (vals[c + k, z, i] for k in range(3))
                    line.append(three(u * u, v * v, w * w))
                filtered.append([three(*line[i : i + 3]) for i in range(count)])
                store(z - 1)
            store(depth - 1)
            store(depth)

        for c in range(5):
            energies(c)

        weigh(depth, blocks, vals, cent, energy, scale, (out, low, high), *sums)

    return kernel


def weigh(depth, blocks, vals, cent, energy, scale, outs, top, total, weighted):
    begin, end = 0, depth
    for z in range(end - begin):
        for i in range(blocks):
            for ref in (top, total, weighted):
                ref[z, i] = jnp.zeros((SUBS, LANES), jnp.float32)

    def offsets(a, b, group):
        first, last = max(0, -a, begin - 1), min(depth, depth - a, end + 1)
        planes = sorted({c + k for c in group for k in range(3)})
        filtered = {}

        def emit(z):
            if not first <= z < last:
                return
            lines = {c: [] for c in group}
            for i in range(blocks + 2):
                v = {k: vals[k, z + a, i + b] for k in planes}
                m = [cent[k, z, i] for k in range(3)]
                for c in group:
                    lines[c].append(m[0] * v[c] + m[2] * v[c + 2] + m[1] * v[c + 1])
            filtered[z] = {
                c: [three(*lines[c][i : i + 3]) for i in range(blocks)] for c in group
            }

        emit(begin - 1)
        emit(begin)
        for z in range(begin, end):
            emit(z + 1)
            for i in range(blocks):
                weights = {}
                for c in group:
                    parts = [filtered[y][c][i] for y in (z - 1, z + 1) if y in filtered]
                    if z in filtered:
                        parts.append(GAIN * filtered[z][c][i])
                    if -1 <= z + a <= depth:
                        parts.append(energy[c, z + a + 1, i + b])
                    if parts:
                        weights[c] = jnp.exp2(scale[z, i] * sum(parts[1:], parts[0]))
                    else:
                        weights[c] = jnp.ones((SUBS, LANES), jnp.float32)
                t = top[z - begin, i]
                s = total[z - begin, i]
                for c in group:
                    t = jnp.maximum(t, weights[c])
                    s = s + weights[c]
                top[z - begin, i] = t
                total[z - begin, i] = s
                if 0 <= z + a < depth:
                    w = weighted[z - begin, i]
                    for c in group:
                        w = w + weights[c] * vals[c + 1, z + a, i + b + 1]
                    weighted[z - begin, i] = w

    for a in range(-2, 3):

        def one(n, _, a=a):
            b = n + jnp.where(n >= 2, 1, 0) if a == 0 else n
            offsets(a, b, range(5))
            return 0

        lax.fori_loop(0, 4 if a == 0 else 5, one, 0)
    offsets(0, 2, (0, 1, 3, 4))

    for z in range(end - begin):
        for i in range(blocks):
            t = top[z, i]
            value = (weighted[z, i] + t * vals[3, z + begin, i + 3]) / (total[z, i] + t)
            part = outs[1 + z // (depth // 2)]
            for ref, at in ((outs[0], z), (part, z % (depth // 2))):
                ref[at, pl.ds(i, SUBS, stride=blocks), :] = value


def place_kernel(sources, rows):
    def kernel(*refs):
        parts, (*_, out, done) = refs[: len(sources)], refs[len(sources) :]
        off = lax.axis_index("off")
        copies = []
        for n, (part, (step, z)) in enumerate(zip(parts, sources)):
            at = pl.ds(pl.multiple_of((off ^ step) * rows, SUBS), rows)
            target = out.at[z : z + part.shape[0], at, :]
            copies.append(pltpu.make_async_copy(part, target, done.at[n]))
            copies[n].start()
        for copy in copies:
            copy.wait()

    return kernel


def shards(volume, strength):
    depth, size_x, size_y = strength.shape
    gxs, gys, offs = (lax.axis_size(axis) for axis in ("gx", "gy", "off"))
    rows = size_x // offs
    blocks = rows // SUBS
    tall = rows + 2 * SUBS
    assert size_y == LANES and offs > 1
    tile = (SUBS, LANES)
    f32 = jnp.float32
    HBM = pl.BlockSpec(memory_space=pltpu.HBM)

    small = pltpu.CompilerParams(vmem_limit_bytes=4 * 2**20)

    def shape(*sizes):
        return jax.ShapeDtypeStruct(sizes, f32)

    layer = pl.pallas_call(
        layer_kernel,
        out_shape=shape(depth, *tile),
        in_specs=[HBM],
        out_specs=VMEM,
        scratch_shapes=[pltpu.SemaphoreType.DMA],
        compiler_params=small,
    )(volume)
    moves = []
    for x in range(gxs):
        for k in range(offs):
            to = (x + (1 if k == 0 else -1)) % gxs
            moves.append((x * offs + k, to * offs + k))
    layer = lax.ppermute(layer, ("gx", "off"), moves)
    strips, mine, scale = pl.pallas_call(
        pack_kernel(rows, size_x),
        out_shape=[shape(tall, LANES), shape(depth, tall, LANES), shape(depth, blocks, *tile)],
        in_specs=[HBM, HBM],
        out_specs=[VMEM] * 3,
        scratch_shapes=[pltpu.VMEM((depth, rows, LANES), f32), pltpu.SemaphoreType.DMA((2,))],
        cost_estimate=pl.CostEstimate(flops=4_000_000, bytes_accessed=4_000_000, transcendentals=0),
        compiler_params=small,
    )(volume, strength)
    strips = pl.pallas_call(
        join_kernel,
        out_shape=shape(tall, LANES),
        in_specs=[VMEM] * 2,
        out_specs=VMEM,
        compiler_params=small,
    )(strips, layer)
    first, second = partners(gys)
    near = lax.ppermute(strips, "gy", list(enumerate(first)))
    far = lax.ppermute(strips, "gy", list(enumerate(second)))
    moved = pl.pallas_call(
        shift_kernel(rows, size_x),
        out_shape=shape(depth, 7, tall, LANES),
        in_specs=[VMEM] * 2,
        out_specs=VMEM,
        cost_estimate=pl.CostEstimate(flops=4_000_000, bytes_accessed=4_000_000, transcendentals=0),
        compiler_params=small,
    )(mine, layer)
    half = depth // 2
    part, *halves = pl.pallas_call(
        main_kernel(depth, rows, blocks),
        out_shape=[shape(depth, rows, size_y)] + [shape(half, rows, size_y)] * 2,
        in_specs=[VMEM] * 4,
        out_specs=[VMEM] * 3,
        scratch_shapes=[
            pltpu.VMEM((depth, 7, tall, LANES), f32),
            pltpu.VMEM((7, depth, blocks + 6) + tile, f32),
            pltpu.VMEM((3, depth, blocks + 2) + tile, f32),
            pltpu.VMEM((5, depth + 2, blocks + 4) + tile, f32),
        ]
        + [pltpu.VMEM((depth, blocks) + tile, f32)] * 3,
        compiler_params=pltpu.CompilerParams(vmem_limit_bytes=16 * 2**20),
    )(moved, scale, near, far)

    def place(blocks, whole, keep=0):
        count = len(blocks)
        held = [] if whole is None else [whole]
        outs = [shape(*block.shape) for _, block in blocks[:keep]]
        return pl.pallas_call(
            place_kernel([source for source, _ in blocks], rows),
            out_shape=outs + [shape(depth, size_x, size_y)],
            in_specs=[VMEM] * count + [HBM] * len(held),
            out_specs=[VMEM] * keep + [HBM],
            scratch_shapes=[pltpu.SemaphoreType.DMA((count,))],
            input_output_aliases={n: n for n in range(keep)} | ({count: keep} if held else {}),
            compiler_params=small,
        )(*(block for _, block in blocks), *held)

    def swapped(block, bit):
        return lax.ppermute(block, "off", [(i, i ^ bit) for i in range(offs)])

    assert offs & (offs - 1) == 0
    bit, ready = 1, [((0, 0), part)]
    while 2 * bit < offs:
        ready += [((step ^ bit, z), swapped(block, bit)) for (step, z), block in ready]
        bit *= 2
    *halves, whole = place([((0, half * n), halves[n]) for n in range(2)], None, keep=2)
    late = [((bit, half * n), swapped(halves[n], bit)) for n in range(2)]
    ready, last = ready[1:] + late, []
    while bit > 1:
        bit //= 2
        last += [((step ^ bit, z), swapped(block, bit)) for (step, z), block in late + last]
    (whole,) = place(ready, whole)
    (whole,) = place(last, whole)
    return whole


def solution(mesh):
    return jax.shard_map(
        shards,
        mesh=mesh,
        in_specs=(P(None, "gx", "gy"), P(None, "gx", "gy")),
        out_specs=P(None, "gx", "gy"),
        check_vma=False,
    )
```

```python
import math

import jax
import jax.numpy as jnp
from jax import lax
from jax.experimental import pallas as pl
from jax.experimental.pallas import tpu as pltpu
from jax.sharding import PartitionSpec as P

EDGE = math.exp(-0.5) / (1.0 + 2.0 * math.exp(-0.5))
GAIN = math.exp(0.5)
SCALE = -(EDGE**3) * math.log2(math.e)
LANES = 128
SUBS = 8
VMEM = pl.BlockSpec(memory_space=pltpu.VMEM)


def partners(count):
    assert count % 2 == 0
    first = [i ^ 1 for i in range(count)]
    second = [(((i + 1) ^ 1) - 1) % count for i in range(count)]
    return first, second


def packed(slices, lane):
    place = (lane + 3) % LANES
    line = jnp.zeros((SUBS, LANES), jnp.float32)
    for z, v in enumerate(slices):
        v = pltpu.roll(v, 16 * z, 1) if z else v
        line = jnp.where((place >= 16 * z) & (place < 16 * z + 6), v, line)
    return line


def lanes():
    return lax.broadcasted_iota(jnp.int32, (SUBS, LANES), 1)


def layer_kernel(volume, layer, arrived):
    off, size_x = lax.axis_index("off"), volume.shape[1]
    at = pl.multiple_of(jnp.where(off == 0, size_x - SUBS, 0), SUBS)
    copy = pltpu.make_async_copy(volume.at[:, pl.ds(at, SUBS), :], layer, arrived)
    copy.start()
    copy.wait()


def window(off, rows, size_x):
    begin = pl.multiple_of(jnp.clip(off * rows - SUBS, 0, size_x - rows - 2 * SUBS), SUBS)

    def block(j):
        at = jnp.clip(off * rows + SUBS * (j - 1), 0, size_x - SUBS) - begin
        return pl.ds(pl.multiple_of(at, SUBS), SUBS)

    return begin, block


def pack_kernel(rows, size_x):
    blocks = rows // SUBS

    def kernel(volume, strength, strips, mine, scale, local, arrived):
        depth = volume.shape[0]
        off = lax.axis_index("off")
        begin, block = window(off, rows, size_x)
        first = pltpu.make_async_copy(
            volume.at[:, pl.ds(begin, rows + 2 * SUBS), :], mine, arrived.at[0]
        )
        start = pl.multiple_of(off * rows, SUBS)
        second = pltpu.make_async_copy(
            strength.at[:, pl.ds(start, rows), :], local, arrived.at[1]
        )
        first.start()
        second.start()
        lane = lanes()
        first.wait()
        for j in range(blocks + 2):
            strips[pl.ds(SUBS * j, SUBS), :] = packed(
                [mine[z, block(j), :] for z in range(depth)], lane
            )
        second.wait()
        for z in range(depth):
            for i in range(blocks):
                scale[z, i] = SCALE / local[z, pl.ds(i, SUBS, stride=blocks), :]

    return kernel


def edges(tall):
    off, offs = lax.axis_index("off"), lax.axis_size("off")
    gx, gxs = lax.axis_index("gx"), lax.axis_size("gx")
    return {0: (off == 0, gx == 0), tall - 1: (off == offs - 1, gx == gxs - 1)}


def join_kernel(strips, layer, joined):
    depth, tall = layer.shape[0], strips.shape[0] // SUBS
    line = packed([layer[z] for z in range(depth)], lanes())
    for j in range(tall):
        at = pl.ds(SUBS * j, SUBS)
        value = strips[at, :]
        for end, (outside, beyond) in edges(tall).items():
            if j == end:
                value = jnp.where(outside, jnp.where(beyond, 0.0, line), value)
        joined[at, :] = value


def three(a, b, c):
    return a + c + GAIN * b


def shift_kernel(rows, size_x):
    def kernel(mine, layer, moved):
        depth, tall = mine.shape[0], mine.shape[1] // SUBS
        _, block = window(lax.axis_index("off"), rows, size_x)
        ends = edges(tall)
        for z in range(depth):
            for r in range(tall):
                v = mine[z, block(r), :]
                if r in ends:
                    v = jnp.where(ends[r][0], jnp.where(ends[r][1], 0.0, layer[z]), v)
                for c in range(7):
                    shift = (3 - c) % LANES
                    moved[z, c, pl.ds(SUBS * r, SUBS), :] = pltpu.roll(v, shift, 1) if shift else v

    return kernel


def main_kernel(depth, rows, blocks):
    wide = blocks + 6
    tall = rows // SUBS + 2

    def kernel(moved, scale, near, far, low, vals, cent, energy, flat, *sums):
        lane = lanes()
        gy, gys = lax.axis_index("gy"), lax.axis_size("gy")
        outer = lane % 16 >= 13
        closed = (outer & (gy == 0)) | ((lane % 16 < 3) & (gy == gys - 1))
        from_near = outer == (gy % 2 == 1)

        def side(j):
            at = pl.ds(SUBS * j, SUBS)
            line = jnp.where(closed, 0.0, jnp.where(from_near, near[at, :], far[at, :]))
            return [
                jnp.where(outer, pltpu.roll(line, LANES - c, 1), pltpu.roll(line, c, 1))
                for c in range(1, 4)
            ]

        lines = [side(j) for j in range(tall)]

        def fill(z):
            for r in range(tall):
                at = pl.ds(SUBS * r, SUBS)
                flat[z, 3, at, :] = moved[z, 3, at, :]
                for c in range(1, 4):
                    h = pltpu.roll(lines[r][c - 1], LANES - 16 * z, 1) if z else lines[r][c - 1]
                    flat[z, 3 + c, at, :] = jnp.where(lane >= LANES - c, h, moved[z, 3 + c, at, :])
                    flat[z, 3 - c, at, :] = jnp.where(lane < c, h, moved[z, 3 - c, at, :])
            for i in range(wide):
                for c in range(7):
                    v = flat[z, c, pl.ds(SUBS - 3 + i, SUBS, stride=blocks), :]
                    vals[c, z, i] = v
                    if 2 <= c <= 4 and 2 <= i < wide - 2:
                        cent[c - 2, z, i - 2] = (-2.0 * GAIN if c == 3 else -2.0) * v

        for z in range(depth):
            fill(z)

        def energies(c):
            count = blocks + 4
            filtered = []

            def store(z):
                for i in range(count):
                    e = GAIN * filtered[z][i] if 0 <= z < depth else None
                    for y in (z - 1, z + 1):
                        if 0 <= y < depth:
                            e = filtered[y][i] if e is None else e + filtered[y][i]
                    energy[c, z + 1, i] = e

            for z in range(depth):
                line = []
                for i in range(wide):
                    u, v, w = (vals[c + k, z, i] for k in range(3))
                    line.append(three(u * u, v * v, w * w))
                filtered.append([three(*line[i : i + 3]) for i in range(count)])
                store(z - 1)
            store(depth - 1)
            store(depth)

        for c in range(5):
            energies(c)

        weigh(depth, blocks, (0, depth // 2), vals, cent, energy, scale, low, *sums)

    return kernel


def second_kernel(depth, blocks):
    def kernel(vals, cent, energy, scale, low, kept, high, *sums):
        kept[...] = low[...]
        weigh(depth, blocks, (depth // 2, depth), vals, cent, energy, scale, high, *sums)

    return kernel


def weigh(depth, blocks, slices, vals, cent, energy, scale, out, top, total, weighted):
    begin, end = slices
    for z in range(end - begin):
        for i in range(blocks):
            for ref in (top, total, weighted):
                ref[z, i] = jnp.zeros((SUBS, LANES), jnp.float32)

    def offsets(a, b, group):
        first, last = max(0, -a, begin - 1), min(depth, depth - a, end + 1)
        planes = sorted({c + k for c in group for k in range(3)})
        filtered = {}

        def emit(z):
            if not first <= z < last:
                return
            lines = {c: [] for c in group}
            for i in range(blocks + 2):
                v = {k: vals[k, z + a, i + b] for k in planes}
                m = [cent[k, z, i] for k in range(3)]
                for c in group:
                    lines[c].append(m[0] * v[c] + m[2] * v[c + 2] + m[1] * v[c + 1])
            filtered[z] = {
                c: [three(*lines[c][i : i + 3]) for i in range(blocks)] for c in group
            }

        emit(begin - 1)
        emit(begin)
        for z in range(begin, end):
            emit(z + 1)
            for i in range(blocks):
                weights = {}
                for c in group:
                    parts = [filtered[y][c][i] for y in (z - 1, z + 1) if y in filtered]
                    if z in filtered:
                        parts.append(GAIN * filtered[z][c][i])
                    if -1 <= z + a <= depth:
                        parts.append(energy[c, z + a + 1, i + b])
                    if parts:
                        weights[c] = jnp.exp2(scale[z, i] * sum(parts[1:], parts[0]))
                    else:
                        weights[c] = jnp.ones((SUBS, LANES), jnp.float32)
                t = top[z - begin, i]
                s = total[z - begin, i]
                for c in group:
                    t = jnp.maximum(t, weights[c])
                    s = s + weights[c]
                top[z - begin, i] = t
                total[z - begin, i] = s
                if 0 <= z + a < depth:
                    w = weighted[z - begin, i]
                    for c in group:
                        w = w + weights[c] * vals[c + 1, z + a, i + b + 1]
                    weighted[z - begin, i] = w

    for a in range(-2, 3):

        def one(n, _, a=a):
            b = n + jnp.where(n >= 2, 1, 0) if a == 0 else n
            offsets(a, b, range(5))
            return 0

        lax.fori_loop(0, 4 if a == 0 else 5, one, 0)
    offsets(0, 2, (0, 1, 3, 4))

    for z in range(end - begin):
        for i in range(blocks):
            t = top[z, i]
            value = (weighted[z, i] + t * vals[3, z + begin, i + 3]) / (total[z, i] + t)
            out[z, pl.ds(i, SUBS, stride=blocks), :] = value


def place_kernel(sources, rows):
    def kernel(*refs):
        parts, (*_, out, done) = refs[: len(sources)], refs[len(sources) :]
        off = lax.axis_index("off")
        copies = []
        for n, (part, (step, z)) in enumerate(zip(parts, sources)):
            at = pl.ds(pl.multiple_of((off ^ step) * rows, SUBS), rows)
            target = out.at[z : z + part.shape[0], at, :]
            copies.append(pltpu.make_async_copy(part, target, done.at[n]))
            copies[n].start()
        for copy in copies:
            copy.wait()

    return kernel


def shards(volume, strength):
    depth, size_x, size_y = strength.shape
    gxs, gys, offs = (lax.axis_size(axis) for axis in ("gx", "gy", "off"))
    rows = size_x // offs
    blocks = rows // SUBS
    tall = rows + 2 * SUBS
    assert size_y == LANES and offs > 1
    tile = (SUBS, LANES)
    f32 = jnp.float32
    HBM = pl.BlockSpec(memory_space=pltpu.HBM)

    small = pltpu.CompilerParams(vmem_limit_bytes=4 * 2**20)

    def shape(*sizes):
        return jax.ShapeDtypeStruct(sizes, f32)

    layer = pl.pallas_call(
        layer_kernel,
        out_shape=shape(depth, *tile),
        in_specs=[HBM],
        out_specs=VMEM,
        scratch_shapes=[pltpu.SemaphoreType.DMA],
        compiler_params=small,
    )(volume)
    moves = []
    for x in range(gxs):
        for k in range(offs):
            to = (x + (1 if k == 0 else -1)) % gxs
            moves.append((x * offs + k, to * offs + k))
    layer = lax.ppermute(layer, ("gx", "off"), moves)
    strips, mine, scale = pl.pallas_call(
        pack_kernel(rows, size_x),
        out_shape=[shape(tall, LANES), shape(depth, tall, LANES), shape(depth, blocks, *tile)],
        in_specs=[HBM, HBM],
        out_specs=[VMEM] * 3,
        scratch_shapes=[pltpu.VMEM((depth, rows, LANES), f32), pltpu.SemaphoreType.DMA((2,))],
        cost_estimate=pl.CostEstimate(flops=4_000_000, bytes_accessed=4_000_000, transcendentals=0),
        compiler_params=small,
    )(volume, strength)
    strips = pl.pallas_call(
        join_kernel,
        out_shape=shape(tall, LANES),
        in_specs=[VMEM] * 2,
        out_specs=VMEM,
        compiler_params=small,
    )(strips, layer)
    first, second = partners(gys)
    near = lax.ppermute(strips, "gy", list(enumerate(first)))
    far = lax.ppermute(strips, "gy", list(enumerate(second)))
    moved = pl.pallas_call(
        shift_kernel(rows, size_x),
        out_shape=shape(depth, 7, tall, LANES),
        in_specs=[VMEM] * 2,
        out_specs=VMEM,
        cost_estimate=pl.CostEstimate(flops=4_000_000, bytes_accessed=4_000_000, transcendentals=0),
        compiler_params=small,
    )(mine, layer)
    half = depth // 2
    sums = [pltpu.VMEM((half, blocks) + tile, f32)] * 3
    large = pltpu.CompilerParams(vmem_limit_bytes=16 * 2**20)
    low, *prepared = pl.pallas_call(
        main_kernel(depth, rows, blocks),
        out_shape=[
            shape(half, rows, size_y),
            shape(7, depth, blocks + 6, *tile),
            shape(3, depth, blocks + 2, *tile),
            shape(5, depth + 2, blocks + 4, *tile),
        ],
        in_specs=[VMEM] * 4,
        out_specs=[VMEM] * 4,
        scratch_shapes=[pltpu.VMEM((depth, 7, tall, LANES), f32)] + sums,
        compiler_params=large,
    )(moved, scale, near, far)
    work = 124 * 20 * half * rows * size_y
    halves = pl.pallas_call(
        second_kernel(depth, blocks),
        out_shape=[shape(half, rows, size_y)] * 2,
        in_specs=[VMEM] * 5,
        out_specs=[VMEM] * 2,
        scratch_shapes=sums,
        cost_estimate=pl.CostEstimate(flops=work, bytes_accessed=work // 2, transcendentals=0),
        compiler_params=large,
    )(*prepared, scale, low)

    def place(blocks, whole):
        count = len(blocks)
        held = [] if whole is None else [whole]
        return pl.pallas_call(
            place_kernel([source for source, _ in blocks], rows),
            out_shape=shape(depth, size_x, size_y),
            in_specs=[VMEM] * count + [HBM] * len(held),
            out_specs=HBM,
            scratch_shapes=[pltpu.SemaphoreType.DMA((count,))],
            input_output_aliases={count: 0} if held else {},
            compiler_params=small,
        )(*(block for _, block in blocks), *held)

    def swapped(block, bit):
        return lax.ppermute(block, "off", [(i, i ^ bit) for i in range(offs)])

    assert offs & (offs - 1) == 0
    bit = offs // 2
    arrived = swapped(low, bit)
    low, high, arrived = lax.optimization_barrier((*halves, arrived))
    blocks = [((0, 0), low), ((0, half), high), ((bit, 0), arrived), ((bit, half), swapped(high, bit))]
    while bit > 1:
        bit //= 2
        blocks += [((step ^ bit, z), swapped(block, bit)) for (step, z), block in blocks]
    return place(blocks[-2:], place(blocks[:-2], None))


def solution(mesh):
    return jax.shard_map(
        shards,
        mesh=mesh,
        in_specs=(P(None, "gx", "gy"), P(None, "gx", "gy")),
        out_specs=P(None, "gx", "gy"),
        check_vma=False,
    )
```

```python
import math

import jax
import jax.numpy as jnp
from jax import lax
from jax.experimental import pallas as pl
from jax.experimental.pallas import tpu as pltpu
from jax.sharding import PartitionSpec as P

EDGE = math.exp(-0.5) / (1.0 + 2.0 * math.exp(-0.5))
GAIN = math.exp(0.5)
SCALE = -(EDGE**3) * math.log2(math.e)
LANES = 128
SUBS = 8
VMEM = pl.BlockSpec(memory_space=pltpu.VMEM)


def partners(count):
    assert count % 2 == 0
    first = [i ^ 1 for i in range(count)]
    second = [(((i + 1) ^ 1) - 1) % count for i in range(count)]
    return first, second


def packed(slices, lane):
    place = (lane + 3) % LANES
    line = jnp.zeros((SUBS, LANES), jnp.float32)
    for z, v in enumerate(slices):
        v = pltpu.roll(v, 16 * z, 1) if z else v
        line = jnp.where((place >= 16 * z) & (place < 16 * z + 6), v, line)
    return line


def lanes():
    return lax.broadcasted_iota(jnp.int32, (SUBS, LANES), 1)


def layer_kernel(volume, layer, arrived):
    off, size_x = lax.axis_index("off"), volume.shape[1]
    at = pl.multiple_of(jnp.where(off == 0, size_x - SUBS, 0), SUBS)
    copy = pltpu.make_async_copy(volume.at[:, pl.ds(at, SUBS), :], layer, arrived)
    copy.start()
    copy.wait()


def window(off, rows, size_x):
    begin = pl.multiple_of(jnp.clip(off * rows - SUBS, 0, size_x - rows - 2 * SUBS), SUBS)

    def block(j):
        at = jnp.clip(off * rows + SUBS * (j - 1), 0, size_x - SUBS) - begin
        return pl.ds(pl.multiple_of(at, SUBS), SUBS)

    return begin, block


def pack_kernel(rows, size_x):
    blocks = rows // SUBS

    def kernel(volume, strength, strips, mine, scale, local, arrived):
        depth = volume.shape[0]
        off = lax.axis_index("off")
        begin, block = window(off, rows, size_x)
        first = pltpu.make_async_copy(
            volume.at[:, pl.ds(begin, rows + 2 * SUBS), :], mine, arrived.at[0]
        )
        start = pl.multiple_of(off * rows, SUBS)
        second = pltpu.make_async_copy(
            strength.at[:, pl.ds(start, rows), :], local, arrived.at[1]
        )
        first.start()
        second.start()
        lane = lanes()
        first.wait()
        for j in range(blocks + 2):
            strips[pl.ds(SUBS * j, SUBS), :] = packed(
                [mine[z, block(j), :] for z in range(depth)], lane
            )
        second.wait()
        for z in range(depth):
            for i in range(blocks):
                scale[z, i] = SCALE / local[z, pl.ds(i, SUBS, stride=blocks), :]

    return kernel


def edges(tall):
    off, offs = lax.axis_index("off"), lax.axis_size("off")
    gx, gxs = lax.axis_index("gx"), lax.axis_size("gx")
    return {0: (off == 0, gx == 0), tall - 1: (off == offs - 1, gx == gxs - 1)}


def join_kernel(strips, layer, joined):
    depth, tall = layer.shape[0], strips.shape[0] // SUBS
    line = packed([layer[z] for z in range(depth)], lanes())
    for j in range(tall):
        at = pl.ds(SUBS * j, SUBS)
        value = strips[at, :]
        for end, (outside, beyond) in edges(tall).items():
            if j == end:
                value = jnp.where(outside, jnp.where(beyond, 0.0, line), value)
        joined[at, :] = value


def three(a, b, c):
    return a + c + GAIN * b


def shift_kernel(rows, size_x):
    def kernel(mine, layer, moved):
        depth, tall = mine.shape[0], mine.shape[1] // SUBS
        _, block = window(lax.axis_index("off"), rows, size_x)
        ends = edges(tall)
        for z in range(depth):
            for r in range(tall):
                v = mine[z, block(r), :]
                if r in ends:
                    v = jnp.where(ends[r][0], jnp.where(ends[r][1], 0.0, layer[z]), v)
                for c in range(7):
                    shift = (3 - c) % LANES
                    moved[z, c, pl.ds(SUBS * r, SUBS), :] = pltpu.roll(v, shift, 1) if shift else v

    return kernel


def main_kernel(depth, rows, blocks):
    wide = blocks + 6
    tall = rows // SUBS + 2

    def kernel(moved, scale, near, far, low, vals, cent, energy, flat, *sums):
        lane = lanes()
        gy, gys = lax.axis_index("gy"), lax.axis_size("gy")
        outer = lane % 16 >= 13
        closed = (outer & (gy == 0)) | ((lane % 16 < 3) & (gy == gys - 1))
        from_near = outer == (gy % 2 == 1)

        def side(j):
            at = pl.ds(SUBS * j, SUBS)
            line = jnp.where(closed, 0.0, jnp.where(from_near, near[at, :], far[at, :]))
            return [
                jnp.where(outer, pltpu.roll(line, LANES - c, 1), pltpu.roll(line, c, 1))
                for c in range(1, 4)
            ]

        lines = [side(j) for j in range(tall)]

        def fill(z):
            for r in range(tall):
                at = pl.ds(SUBS * r, SUBS)
                flat[z, 3, at, :] = moved[z, 3, at, :]
                for c in range(1, 4):
                    h = pltpu.roll(lines[r][c - 1], LANES - 16 * z, 1) if z else lines[r][c - 1]
                    flat[z, 3 + c, at, :] = jnp.where(lane >= LANES - c, h, moved[z, 3 + c, at, :])
                    flat[z, 3 - c, at, :] = jnp.where(lane < c, h, moved[z, 3 - c, at, :])
            for i in range(wide):
                for c in range(7):
                    v = flat[z, c, pl.ds(SUBS - 3 + i, SUBS, stride=blocks), :]
                    vals[c, z, i] = v
                    if 2 <= c <= 4 and 2 <= i < wide - 2:
                        cent[c - 2, z, i - 2] = (-2.0 * GAIN if c == 3 else -2.0) * v

        for z in range(depth):
            fill(z)

        def energies(c):
            count = blocks + 4
            filtered = []

            def store(z):
                for i in range(count):
                    e = GAIN * filtered[z][i] if 0 <= z < depth else None
                    for y in (z - 1, z + 1):
                        if 0 <= y < depth:
                            e = filtered[y][i] if e is None else e + filtered[y][i]
                    energy[c, z + 1, i] = e

            for z in range(depth):
                line = []
                for i in range(wide):
                    u, v, w = (vals[c + k, z, i] for k in range(3))
                    line.append(three(u * u, v * v, w * w))
                filtered.append([three(*line[i : i + 3]) for i in range(count)])
                store(z - 1)
            store(depth - 1)
            store(depth)

        for c in range(5):
            energies(c)

        weigh(depth, blocks, (0, depth // 2), vals, cent, energy, scale, low, *sums)

    return kernel


def second_kernel(depth, blocks):
    def kernel(vals, cent, energy, scale, low, kept, high, *sums):
        kept[...] = low[...]
        weigh(depth, blocks, (depth // 2, depth), vals, cent, energy, scale, high, *sums)

    return kernel


def weigh(depth, blocks, slices, vals, cent, energy, scale, out, top, total, weighted):
    begin, end = slices
    for z in range(end - begin):
        for i in range(blocks):
            for ref in (top, total, weighted):
                ref[z, i] = jnp.zeros((SUBS, LANES), jnp.float32)

    def offsets(a, b, group):
        first, last = max(0, -a, begin - 1), min(depth, depth - a, end + 1)
        planes = sorted({c + k for c in group for k in range(3)})
        filtered = {}

        def emit(z):
            if not first <= z < last:
                return
            lines = {c: [] for c in group}
            for i in range(blocks + 2):
                v = {k: vals[k, z + a, i + b] for k in planes}
                m = [cent[k, z, i] for k in range(3)]
                for c in group:
                    lines[c].append(m[0] * v[c] + m[2] * v[c + 2] + m[1] * v[c + 1])
            filtered[z] = {
                c: [three(*lines[c][i : i + 3]) for i in range(blocks)] for c in group
            }

        emit(begin - 1)
        emit(begin)
        for z in range(begin, end):
            emit(z + 1)
            for i in range(blocks):
                weights = {}
                for c in group:
                    parts = [filtered[y][c][i] for y in (z - 1, z + 1) if y in filtered]
                    if z in filtered:
                        parts.append(GAIN * filtered[z][c][i])
                    if -1 <= z + a <= depth:
                        parts.append(energy[c, z + a + 1, i + b])
                    if parts:
                        weights[c] = jnp.exp2(scale[z, i] * sum(parts[1:], parts[0]))
                    else:
                        weights[c] = jnp.ones((SUBS, LANES), jnp.float32)
                t = top[z - begin, i]
                s = total[z - begin, i]
                for c in group:
                    t = jnp.maximum(t, weights[c])
                    s = s + weights[c]
                top[z - begin, i] = t
                total[z - begin, i] = s
                if 0 <= z + a < depth:
                    w = weighted[z - begin, i]
                    for c in group:
                        w = w + weights[c] * vals[c + 1, z + a, i + b + 1]
                    weighted[z - begin, i] = w

    for a in range(-2, 3):

        def one(n, _, a=a):
            b = n + jnp.where(n >= 2, 1, 0) if a == 0 else n
            offsets(a, b, range(5))
            return 0

        lax.fori_loop(0, 4 if a == 0 else 5, one, 0)
    offsets(0, 2, (0, 1, 3, 4))

    for z in range(end - begin):
        for i in range(blocks):
            t = top[z, i]
            value = (weighted[z, i] + t * vals[3, z + begin, i + 3]) / (total[z, i] + t)
            out[z, pl.ds(i, SUBS, stride=blocks), :] = value


def place_kernel(sources, rows, slices):
    def kernel(*refs):
        parts, (*_, out, done) = refs[: len(sources)], refs[len(sources) :]
        off = lax.axis_index("off")
        copies = []
        for n, (part, (step, z, first)) in enumerate(zip(parts, sources)):
            at = pl.ds(pl.multiple_of((off ^ step) * rows, SUBS), rows)
            target = out.at[z : z + slices, at, :]
            part = part.at[first : first + slices]
            copies.append(pltpu.make_async_copy(part, target, done.at[n]))
            copies[n].start()
        for copy in copies:
            copy.wait()

    return kernel


def shards(volume, strength):
    depth, size_x, size_y = strength.shape
    gxs, gys, offs = (lax.axis_size(axis) for axis in ("gx", "gy", "off"))
    rows = size_x // offs
    blocks = rows // SUBS
    tall = rows + 2 * SUBS
    assert size_y == LANES and offs > 1
    tile = (SUBS, LANES)
    f32 = jnp.float32
    HBM = pl.BlockSpec(memory_space=pltpu.HBM)

    small = pltpu.CompilerParams(vmem_limit_bytes=4 * 2**20)

    def shape(*sizes):
        return jax.ShapeDtypeStruct(sizes, f32)

    layer = pl.pallas_call(
        layer_kernel,
        out_shape=shape(depth, *tile),
        in_specs=[HBM],
        out_specs=VMEM,
        scratch_shapes=[pltpu.SemaphoreType.DMA],
        compiler_params=small,
    )(volume)
    moves = []
    for x in range(gxs):
        for k in range(offs):
            to = (x + (1 if k == 0 else -1)) % gxs
            moves.append((x * offs + k, to * offs + k))
    layer = lax.ppermute(layer, ("gx", "off"), moves)
    strips, mine, scale = pl.pallas_call(
        pack_kernel(rows, size_x),
        out_shape=[shape(tall, LANES), shape(depth, tall, LANES), shape(depth, blocks, *tile)],
        in_specs=[HBM, HBM],
        out_specs=[VMEM] * 3,
        scratch_shapes=[pltpu.VMEM((depth, rows, LANES), f32), pltpu.SemaphoreType.DMA((2,))],
        cost_estimate=pl.CostEstimate(flops=4_000_000, bytes_accessed=4_000_000, transcendentals=0),
        compiler_params=small,
    )(volume, strength)
    strips = pl.pallas_call(
        join_kernel,
        out_shape=shape(tall, LANES),
        in_specs=[VMEM] * 2,
        out_specs=VMEM,
        compiler_params=small,
    )(strips, layer)
    first, second = partners(gys)
    near = lax.ppermute(strips, "gy", list(enumerate(first)))
    far = lax.ppermute(strips, "gy", list(enumerate(second)))
    moved = pl.pallas_call(
        shift_kernel(rows, size_x),
        out_shape=shape(depth, 7, tall, LANES),
        in_specs=[VMEM] * 2,
        out_specs=VMEM,
        cost_estimate=pl.CostEstimate(flops=4_000_000, bytes_accessed=4_000_000, transcendentals=0),
        compiler_params=small,
    )(mine, layer)
    half = depth // 2
    sums = [pltpu.VMEM((half, blocks) + tile, f32)] * 3
    large = pltpu.CompilerParams(vmem_limit_bytes=16 * 2**20)
    low, *prepared = pl.pallas_call(
        main_kernel(depth, rows, blocks),
        out_shape=[
            shape(half, rows, size_y),
            shape(7, depth, blocks + 6, *tile),
            shape(3, depth, blocks + 2, *tile),
            shape(5, depth + 2, blocks + 4, *tile),
        ],
        in_specs=[VMEM] * 4,
        out_specs=[VMEM] * 4,
        scratch_shapes=[pltpu.VMEM((depth, 7, tall, LANES), f32)] + sums,
        compiler_params=large,
    )(moved, scale, near, far)
    work = 124 * 20 * half * rows * size_y
    halves = pl.pallas_call(
        second_kernel(depth, blocks),
        out_shape=[shape(half, rows, size_y)] * 2,
        in_specs=[VMEM] * 5,
        out_specs=[VMEM] * 2,
        scratch_shapes=sums,
        cost_estimate=pl.CostEstimate(flops=work, bytes_accessed=work // 2, transcendentals=0),
        compiler_params=large,
    )(*prepared, scale, low)

    def place(blocks, whole):
        count = len(blocks)
        held = [] if whole is None else [whole]
        return pl.pallas_call(
            place_kernel([source for source, _ in blocks], rows, half),
            out_shape=shape(depth, size_x, size_y),
            in_specs=[VMEM] * count + [HBM] * len(held),
            out_specs=HBM,
            scratch_shapes=[pltpu.SemaphoreType.DMA((count,))],
            input_output_aliases={count: 0} if held else {},
            compiler_params=small,
        )(*(block for _, block in blocks), *held)

    def swapped(block, bit):
        return lax.ppermute(block, "off", [(i, i ^ bit) for i in range(offs)])

    assert offs & (offs - 1) == 0
    bit = offs // 2
    arrived = swapped(low, bit)
    low, high, arrived = lax.optimization_barrier((*halves, arrived))
    early = [((0, 0, 0), low), ((0, half, 0), high), ((bit, 0, 0), arrived)]
    late = [((bit, half, 0), swapped(high, bit))]
    while bit > 1:
        bit //= 2
        joined = [block[first : first + half] for (*_, first), block in early]
        got = swapped(jnp.concatenate(joined), bit)
        early += [((at[0] ^ bit, at[1], half * n), got) for n, (at, _) in enumerate(early)]
        last = [((step ^ bit, z, 0), swapped(block, bit)) for (step, z, _), block in late]
        late += last
    return place(late[-1:], place(early + late[:-1], None))


def solution(mesh):
    return jax.shard_map(
        shards,
        mesh=mesh,
        in_specs=(P(None, "gx", "gy"), P(None, "gx", "gy")),
        out_specs=P(None, "gx", "gy"),
        check_vma=False,
    )
```

```python
import math

import jax
import jax.numpy as jnp
from jax import lax
from jax.experimental import pallas as pl
from jax.experimental.pallas import tpu as pltpu
from jax.sharding import PartitionSpec as P

EDGE = math.exp(-0.5) / (1.0 + 2.0 * math.exp(-0.5))
GAIN = math.exp(0.5)
SCALE = -(EDGE**3) * math.log2(math.e)
LANES = 128
SUBS = 8
VMEM = pl.BlockSpec(memory_space=pltpu.VMEM)


def partners(count):
    assert count % 2 == 0
    first = [i ^ 1 for i in range(count)]
    second = [(((i + 1) ^ 1) - 1) % count for i in range(count)]
    return first, second


def packed(slices, lane):
    place = (lane + 3) % LANES
    line = jnp.zeros((SUBS, LANES), jnp.float32)
    for z, v in enumerate(slices):
        v = pltpu.roll(v, 16 * z, 1) if z else v
        line = jnp.where((place >= 16 * z) & (place < 16 * z + 6), v, line)
    return line


def lanes():
    return lax.broadcasted_iota(jnp.int32, (SUBS, LANES), 1)


def window(off, rows, size_x):
    begin = pl.multiple_of(jnp.clip(off * rows - SUBS, 0, size_x - rows - 2 * SUBS), SUBS)

    def block(j):
        at = jnp.clip(off * rows + SUBS * (j - 1), 0, size_x - SUBS) - begin
        return pl.ds(pl.multiple_of(at, SUBS), SUBS)

    return begin, block


def pack_kernel(rows, size_x):
    blocks = rows // SUBS

    def kernel(volume, strength, strips, mine, scale, local, arrived):
        depth = volume.shape[0]
        off = lax.axis_index("off")
        begin, block = window(off, rows, size_x)
        first = pltpu.make_async_copy(
            volume.at[:, pl.ds(begin, rows + 2 * SUBS), :], mine, arrived.at[0]
        )
        start = pl.multiple_of(off * rows, SUBS)
        second = pltpu.make_async_copy(
            strength.at[:, pl.ds(start, rows), :], local, arrived.at[1]
        )
        first.start()
        second.start()
        lane = lanes()
        first.wait()
        for j in range(blocks + 2):
            strips[pl.ds(SUBS * j, SUBS), :] = packed(
                [mine[z, block(j), :] for z in range(depth)], lane
            )
        second.wait()
        for z in range(depth):
            for i in range(blocks):
                scale[z, i] = SCALE / local[z, pl.ds(i, SUBS, stride=blocks), :]

    return kernel


def edges(tall):
    off, offs = lax.axis_index("off"), lax.axis_size("off")
    gx, gxs = lax.axis_index("gx"), lax.axis_size("gx")
    return {0: (off == 0, gx == 0), tall - 1: (off == offs - 1, gx == gxs - 1)}


def join_kernel(strips, layer, joined):
    depth, tall = layer.shape[0], strips.shape[0] // SUBS
    line = packed([layer[z] for z in range(depth)], lanes())
    for j in range(tall):
        at = pl.ds(SUBS * j, SUBS)
        value = strips[at, :]
        for end, (outside, beyond) in edges(tall).items():
            if j == end:
                value = jnp.where(outside, jnp.where(beyond, 0.0, line), value)
        joined[at, :] = value


def three(a, b, c):
    return a + c + GAIN * b


def shift_kernel(rows, size_x):
    def kernel(mine, layer, moved):
        depth, tall = mine.shape[0], mine.shape[1] // SUBS
        _, block = window(lax.axis_index("off"), rows, size_x)
        ends = edges(tall)
        for z in range(depth):
            for r in range(tall):
                v = mine[z, block(r), :]
                if r in ends:
                    v = jnp.where(ends[r][0], jnp.where(ends[r][1], 0.0, layer[z]), v)
                for c in range(7):
                    shift = (3 - c) % LANES
                    moved[z, c, pl.ds(SUBS * r, SUBS), :] = pltpu.roll(v, shift, 1) if shift else v

    return kernel


def main_kernel(depth, rows, blocks):
    wide = blocks + 6
    tall = rows // SUBS + 2

    def kernel(moved, scale, near, far, low, high, flat, vals, cent, energy, *sums):
        lane = lanes()
        gy, gys = lax.axis_index("gy"), lax.axis_size("gy")
        outer = lane % 16 >= 13
        closed = (outer & (gy == 0)) | ((lane % 16 < 3) & (gy == gys - 1))
        from_near = outer == (gy % 2 == 1)

        def side(j):
            at = pl.ds(SUBS * j, SUBS)
            line = jnp.where(closed, 0.0, jnp.where(from_near, near[at, :], far[at, :]))
            return [
                jnp.where(outer, pltpu.roll(line, LANES - c, 1), pltpu.roll(line, c, 1))
                for c in range(1, 4)
            ]

        lines = [side(j) for j in range(tall)]

        def fill(z):
            for r in range(tall):
                at = pl.ds(SUBS * r, SUBS)
                flat[z, 3, at, :] = moved[z, 3, at, :]
                for c in range(1, 4):
                    h = pltpu.roll(lines[r][c - 1], LANES - 16 * z, 1) if z else lines[r][c - 1]
                    flat[z, 3 + c, at, :] = jnp.where(lane >= LANES - c, h, moved[z, 3 + c, at, :])
                    flat[z, 3 - c, at, :] = jnp.where(lane < c, h, moved[z, 3 - c, at, :])
            for i in range(wide):
                for c in range(7):
                    v = flat[z, c, pl.ds(SUBS - 3 + i, SUBS, stride=blocks), :]
                    vals[c, z, i] = v
                    if 2 <= c <= 4 and 2 <= i < wide - 2:
                        cent[c - 2, z, i - 2] = (-2.0 * GAIN if c == 3 else -2.0) * v

        for z in range(depth):
            fill(z)

        def energies(c):
            count = blocks + 4
            filtered = []

            def store(z):
                for i in range(count):
                    e = GAIN * filtered[z][i] if 0 <= z < depth else None
                    for y in (z - 1, z + 1):
                        if 0 <= y < depth:
                            e = filtered[y][i] if e is None else e + filtered[y][i]
                    energy[c, z + 1, i] = e

            for z in range(depth):
                line = []
                for i in range(wide):
                    u, v, w = (vals[c + k, z, i] for k in range(3))
                    line.append(three(u * u, v * v, w * w))
                filtered.append([three(*line[i : i + 3]) for i in range(count)])
                store(z - 1)
            store(depth - 1)
            store(depth)

        for c in range(5):
            energies(c)

        weigh(depth, blocks, vals, cent, energy, scale, (low, high), *sums)

    return kernel


def weigh(depth, blocks, vals, cent, energy, scale, outs, top, total, weighted):
    begin, end = 0, depth
    for z in range(end - begin):
        for i in range(blocks):
            for ref in (top, total, weighted):
                ref[z, i] = jnp.zeros((SUBS, LANES), jnp.float32)

    def offsets(a, b, group):
        first, last = max(0, -a, begin - 1), min(depth, depth - a, end + 1)
        planes = sorted({c + k for c in group for k in range(3)})
        filtered = {}

        def emit(z):
            if not first <= z < last:
                return
            lines = {c: [] for c in group}
            for i in range(blocks + 2):
                v = {k: vals[k, z + a, i + b] for k in planes}
                m = [cent[k, z, i] for k in range(3)]
                for c in group:
                    lines[c].append(m[0] * v[c] + m[2] * v[c + 2] + m[1] * v[c + 1])
            filtered[z] = {
                c: [three(*lines[c][i : i + 3]) for i in range(blocks)] for c in group
            }

        emit(begin - 1)
        emit(begin)
        for z in range(begin, end):
            emit(z + 1)
            for i in range(blocks):
                weights = {}
                for c in group:
                    parts = [filtered[y][c][i] for y in (z - 1, z + 1) if y in filtered]
                    if z in filtered:
                        parts.append(GAIN * filtered[z][c][i])
                    if -1 <= z + a <= depth:
                        parts.append(energy[c, z + a + 1, i + b])
                    if parts:
                        weights[c] = jnp.exp2(scale[z, i] * sum(parts[1:], parts[0]))
                    else:
                        weights[c] = jnp.ones((SUBS, LANES), jnp.float32)
                t = top[z - begin, i]
                s = total[z - begin, i]
                for c in group:
                    t = jnp.maximum(t, weights[c])
                    s = s + weights[c]
                top[z - begin, i] = t
                total[z - begin, i] = s
                if 0 <= z + a < depth:
                    w = weighted[z - begin, i]
                    for c in group:
                        w = w + weights[c] * vals[c + 1, z + a, i + b + 1]
                    weighted[z - begin, i] = w

    for a in range(-2, 3):

        def one(n, _, a=a):
            b = n + jnp.where(n >= 2, 1, 0) if a == 0 else n
            offsets(a, b, range(5))
            return 0

        lax.fori_loop(0, 4 if a == 0 else 5, one, 0)
    offsets(0, 2, (0, 1, 3, 4))

    for z in range(end - begin):
        for i in range(blocks):
            t = top[z, i]
            value = (weighted[z, i] + t * vals[3, z + begin, i + 3]) / (total[z, i] + t)
            part = outs[z // (depth // 2)]
            part[z % (depth // 2), pl.ds(i, SUBS, stride=blocks), :] = value


def place_kernel(sources, rows):
    def kernel(*refs):
        parts, (*_, out, done) = refs[: len(sources)], refs[len(sources) :]
        off = lax.axis_index("off")
        copies = []
        for n, (part, (step, z)) in enumerate(zip(parts, sources)):
            at = pl.ds(pl.multiple_of((off ^ step) * rows, SUBS), rows)
            target = out.at[z : z + part.shape[0], at, :]
            copies.append(pltpu.make_async_copy(part, target, done.at[n]))
            copies[n].start()
        for copy in copies:
            copy.wait()

    return kernel


def shards(volume, strength):
    depth, size_x, size_y = strength.shape
    gxs, gys, offs = (lax.axis_size(axis) for axis in ("gx", "gy", "off"))
    rows = size_x // offs
    blocks = rows // SUBS
    tall = rows + 2 * SUBS
    assert size_y == LANES and offs > 1
    tile = (SUBS, LANES)
    f32 = jnp.float32
    HBM = pl.BlockSpec(memory_space=pltpu.HBM)

    small = pltpu.CompilerParams(vmem_limit_bytes=4 * 2**20)

    def shape(*sizes):
        return jax.ShapeDtypeStruct(sizes, f32)

    at = jnp.where(lax.axis_index("off") == 0, size_x - SUBS, 0)
    layer = lax.dynamic_slice_in_dim(volume, at, SUBS, 1)
    moves = []
    for x in range(gxs):
        for k in range(offs):
            to = (x + (1 if k == 0 else -1)) % gxs
            moves.append((x * offs + k, to * offs + k))
    layer = lax.ppermute(layer, ("gx", "off"), moves)
    strips, mine, scale = pl.pallas_call(
        pack_kernel(rows, size_x),
        out_shape=[shape(tall, LANES), shape(depth, tall, LANES), shape(depth, blocks, *tile)],
        in_specs=[HBM, HBM],
        out_specs=[VMEM] * 3,
        scratch_shapes=[pltpu.VMEM((depth, rows, LANES), f32), pltpu.SemaphoreType.DMA((2,))],
        cost_estimate=pl.CostEstimate(flops=4_000_000, bytes_accessed=4_000_000, transcendentals=0),
        compiler_params=small,
    )(volume, strength)
    strips = pl.pallas_call(
        join_kernel,
        out_shape=shape(tall, LANES),
        in_specs=[VMEM] * 2,
        out_specs=VMEM,
        compiler_params=small,
    )(strips, layer)
    first, second = partners(gys)
    near = lax.ppermute(strips, "gy", list(enumerate(first)))
    far = lax.ppermute(strips, "gy", list(enumerate(second)))
    moved = pl.pallas_call(
        shift_kernel(rows, size_x),
        out_shape=shape(depth, 7, tall, LANES),
        in_specs=[VMEM] * 2,
        out_specs=VMEM,
        cost_estimate=pl.CostEstimate(flops=4_000_000, bytes_accessed=4_000_000, transcendentals=0),
        compiler_params=small,
    )(mine, layer)
    half = depth // 2
    halves = pl.pallas_call(
        main_kernel(depth, rows, blocks),
        out_shape=[shape(half, rows, size_y)] * 2,
        in_specs=[VMEM] * 4,
        out_specs=[VMEM] * 2,
        scratch_shapes=[
            pltpu.VMEM((depth, 7, tall, LANES), f32),
            pltpu.VMEM((7, depth, blocks + 6) + tile, f32),
            pltpu.VMEM((3, depth, blocks + 2) + tile, f32),
            pltpu.VMEM((5, depth + 2, blocks + 4) + tile, f32),
        ]
        + [pltpu.VMEM((depth, blocks) + tile, f32)] * 3,
        compiler_params=pltpu.CompilerParams(vmem_limit_bytes=16 * 2**20),
    )(moved, scale, near, far)

    def place(blocks, whole):
        count = len(blocks)
        held = [] if whole is None else [whole]
        return pl.pallas_call(
            place_kernel([source for source, _ in blocks], rows),
            out_shape=shape(depth, size_x, size_y),
            in_specs=[VMEM] * count + [HBM] * len(held),
            out_specs=HBM,
            scratch_shapes=[pltpu.SemaphoreType.DMA((count,))],
            input_output_aliases={count: 0} if held else {},
            compiler_params=small,
        )(*(block for _, block in blocks), *held)

    def swapped(block, bit):
        return lax.ppermute(block, "off", [(i, i ^ bit) for i in range(offs)])

    assert offs & (offs - 1) == 0
    bit = offs // 2
    blocks = [((0, half * n), halves[n]) for n in range(2)]
    blocks += [((bit, half * n), swapped(halves[n], bit)) for n in range(2)]
    while bit > 1:
        bit //= 2
        blocks += [((step ^ bit, z), swapped(block, bit)) for (step, z), block in blocks]
    return place(blocks[-2:], place(blocks[:-2], None))


def solution(mesh):
    return jax.shard_map(
        shards,
        mesh=mesh,
        in_specs=(P(None, "gx", "gy"), P(None, "gx", "gy")),
        out_specs=P(None, "gx", "gy"),
        check_vma=False,
    )
```
